512 devices in a mesh: mesh: 128 (over z, x, core), col: 4 (over y).
Axes of the slice: x: 4, y: 4, z: 16, core: 2. Of those that a mesh axis runs over, the one named last changes fastest.
Arguments:
- x_cols: bfloat16 [32, 131072], P('col', 'mesh'), may hold values from -6 to 6
- q_tiles: bfloat16 [5120, 128, 128], P('mesh'), may hold values from -0.25 to 0.25
- q_cols: int32 [1024, 5], P('mesh'), may hold values from 0 to 15, as said below
- halo_ids: int32 [128, 2], P('mesh'), may hold values from 0 to 7
- a_tiles: bfloat16 [8192, 128, 128], P('mesh'), may hold values from -0.1875 to 0.1875
- obs_prec: bfloat16 [8192, 128], P('mesh'), may hold values from 0.5 to 4
- tile_owner: int32 [8192, 1], P('mesh'), may hold values from 0 to 127; in each aligned block of 64 rows (0 to 63, 64 to 127, ...) at most 2 rows name the same one
- tile_sub: int32 [8192], P('mesh'), may hold values from 0 to 7
Outputs:
- product: float32 [32, 131072], P('col', 'mesh')
- gram: float32 [32, 32], P(None, 'col')
The draws below stay inside these ranges and needn't reach their ends.
Inputs may be any that keep to these rules, and one draw needn't show every extreme that they name: `q_cols`: slot values index a partition's window of 16 row blocks as the first step defines. `tile_owner`: among the 64 tiles of one partition, no partition is named more than 2 times.
All inputs are finite; a program needn't handle non-finite values.
Results may differ from the reference program's by a relative error of at most 0.00081.
Values may be sent and summed in bfloat16 or wider, within the bound.
A program may use at most 64 MiB of HBM per device.

```python
import math
import jax
import jax.numpy as jnp
import numpy as np
from jax import lax

TB = 128
COLS = 32
NB = 5
HALO = 2
RB_DEV = 8
OT_DEV = 64
PARTITIONS = 128
ROWBLOCKS = 1024
NODES = 131072
OBS_TILES = 8192
CAP = 2


def draw_q_cols(key, part):
    key_rotate, key_loose = jax.random.split(key, 2)
    row_ids = jnp.arange(ROWBLOCKS, dtype=jnp.int32)
    local_rows = row_ids % RB_DEV
    partition = row_ids // RB_DEV
    rotate = jax.random.randint(key_rotate, (PARTITIONS,), 0, 4 * HALO).astype(jnp.int32)[partition]
    entries = jnp.arange(1, NB, dtype=jnp.int32)
    order_idx = local_rows[:, None] * (NB - 1) + entries[None, :] - 1
    covered = RB_DEV + (order_idx + rotate[:, None]) % (4 * HALO)
    loose = jax.random.randint(key_loose, (ROWBLOCKS, NB - 1), 0, RB_DEV + 4 * HALO).astype(jnp.int32)
    extras = jnp.where(order_idx < 4 * HALO, covered, loose)
    return jnp.concatenate([local_rows[:, None], extras], axis=1).astype(jnp.int32)


def place_ends(result, rng, low, largest):
    spot = [jax.random.randint(jax.random.fold_in(rng, axis), (), 0, length) for axis, length in enumerate(result.shape)]
    main_axis = result.shape.index(max(result.shape))
    beside = spot[:main_axis] + [(spot[main_axis] + 1) % result.shape[main_axis]] + spot[main_axis + 1:]
    return result.at[tuple(spot)].set(low).at[tuple(beside)].set(largest)


def block_scale(rng, extent, cuts, smallest, largest):
    level, own = 1.0, jax.random.fold_in(rng, 6)
    for position, blocks in cuts:
        steps = jnp.exp(jax.random.uniform(jax.random.fold_in(own, position), (blocks,), jnp.float32, smallest / len(cuts), largest / len(cuts)))
        level = level * jnp.repeat(steps, extent[position] // blocks).reshape([-1 if axis == position else 1 for axis in range(len(extent))])
    return level


def shared_out(key, own, number, rows, amount, top, reach, lean):
    sequence = jax.random.permutation(key, amount)
    heavy_load, common = load_shares(amount, rows * top, reach, lean, True), load_shares(amount, rows * top, reach, lean, False)
    places = jnp.arange(amount)

    def named(sizes, offset_by):
        used = int((sizes > 0).sum())
        fixed = max(1, used // 4)
        passed = fixed + (places - fixed + offset_by * (used - fixed)) % max(1, amount - fixed)
        return jnp.zeros((amount,), jnp.int32).at[sequence[jnp.where(places < fixed, places, passed)]].set(jnp.asarray(sizes, jnp.int32))

    sizes = jnp.where(number % 4 == 0, named(heavy_load, number // 4), named(common, number - number // 4 - 1))
    mixed = jax.random.permutation(jax.random.fold_in(own, 3), amount)
    giver, receiver = mixed[0:amount // 2 * 2:2], mixed[1:amount // 2 * 2:2]
    slack = jnp.minimum(sizes[giver] - 1, reach - sizes[receiver]) // 2
    slack = jnp.where((giver == sequence[0]) | (receiver == sequence[0]) | (sizes[receiver] == 0), 0, jnp.maximum(slack, 0))
    passed = jax.random.randint(jax.random.fold_in(own, 4), (amount // 2,), 0, 1 << 20) % (slack + 1)
    sizes = sizes.at[giver].add(-passed).at[receiver].add(passed)
    members = jnp.searchsorted(jnp.cumsum(sizes), jnp.arange(rows * top), side="right").astype(jnp.int32)
    table = members.reshape(top, rows).T
    table = table[jax.random.permutation(jax.random.fold_in(own, 1), rows)]
    offset_by = jax.random.randint(jax.random.fold_in(own, 2), (rows, 1), 0, top)
    return jnp.take_along_axis(table, (jnp.arange(top)[None, :] + offset_by) % top, axis=1)


def load_shares(count, total, reach, lean, full):
    loads = [(1 << 20) // math.isqrt(standing ** lean) + 1 for standing in range(1, count + 1)]
    largest = reach if full else min(reach, max(-(-total // count), total * loads[0] // sum(loads)))
    least = 1 if total - largest >= count - 1 else 0
    counts, surplus = [largest] + [least] * (count - 1), total - largest - least * (count - 1)
    while surplus > 0:
        movable = [i for i in range(1, count) if counts[i] < largest] or [i for i in range(1, count) if counts[i] < reach]
        pool, budget = sum([loads[i] for i in movable]), surplus
        for i in movable:
            addition = min(reach - counts[i], max(1, budget * loads[i] // pool), surplus)
            counts[i] = counts[i] + addition
            surplus = surplus - addition
    return np.array(counts)


def bell_draw(key, shape, deviation, limit, cuts=(), kind=jnp.bfloat16):
    values = deviation * jax.random.normal(key, shape, jnp.float32)
    if cuts:
        values = values * block_scale(key, shape, cuts, -0.22, 0.18)
    return jnp.clip(values, -limit, limit).astype(kind)


def setup_inputs(seed: int = 0) -> dict:
    arg_keys = jax.random.split(jax.random.key(seed), 9)
    x_cols = bell_draw(arg_keys[0], (COLS, NODES), 1.0, 6.0, ((0, 4), (1, 128)))
    q_tiles = bell_draw(arg_keys[1], (ROWBLOCKS * NB, TB, TB), (NB * TB) ** -0.5, 0.25, ((0, 128),))
    q_cols = draw_q_cols(jax.random.fold_in(arg_keys[8], 71), 0)
    halo_ids = place_ends(jax.random.randint(arg_keys[3], (PARTITIONS, HALO), 0, RB_DEV), jax.random.fold_in(arg_keys[3], 1), 0, RB_DEV - 1).astype(jnp.int32)
    a_tiles = bell_draw(arg_keys[4], (OBS_TILES, TB, TB), (8 * TB) ** -0.5, 0.1875, ((0, 128),))
    obs_prec = jnp.clip(jnp.exp(math.log(4.0) - 2.0794415 * jax.random.uniform(arg_keys[5], (OBS_TILES, TB), jnp.float32) ** block_scale(arg_keys[5], (OBS_TILES, TB), ((0, 128),), -0.2, 0.2)), 0.5, 4.0).astype(jnp.bfloat16)
    tile_owner_keys = jax.random.split(jax.random.fold_in(arg_keys[6], 1), OBS_TILES // OT_DEV)
    tile_owner_turns = jax.random.permutation(jax.random.fold_in(arg_keys[6], 3), OBS_TILES // OT_DEV)
    tile_owner = jax.vmap(lambda own, number: shared_out(jax.random.fold_in(arg_keys[6], 2), own, number, OT_DEV, PARTITIONS, 1, CAP, 2))(tile_owner_keys, tile_owner_turns).reshape((OBS_TILES, 1))
    tile_sub = place_ends(jax.random.randint(arg_keys[7], (OBS_TILES,), 0, RB_DEV), jax.random.fold_in(arg_keys[7], 1), 0, RB_DEV - 1).astype(jnp.int32)
    return {"x_cols": x_cols, "q_tiles": q_tiles, "q_cols": q_cols, "halo_ids": halo_ids, "a_tiles": a_tiles, "obs_prec": obs_prec, "tile_owner": tile_owner, "tile_sub": tile_sub}


HIGHEST = lax.Precision.HIGHEST
OFFSETS = (-2, -1, 1, 2)

def window_blocks(q_cols, halo_ids):
    row_ids = jnp.arange(ROWBLOCKS, dtype=jnp.int32)
    partition = (row_ids // RB_DEV)[:, None]
    beyond = jnp.maximum(q_cols - RB_DEV, 0)
    halo_side = beyond // HALO
    halo_slot = beyond % HALO
    offset = jnp.array(OFFSETS, dtype=jnp.int32)[halo_side]
    source_part = (partition + offset) % PARTITIONS
    remote = source_part * RB_DEV + halo_ids[source_part, halo_slot]
    return jnp.where(q_cols < RB_DEV, partition * RB_DEV + q_cols, remote).astype(jnp.int32)

def tile_terms(obs_tiles, precisions, x_blocks):
    wide_tiles = obs_tiles.astype(jnp.float32)
    projected = jnp.einsum('ton,tcn->tco', wide_tiles, x_blocks.astype(jnp.float32), precision=HIGHEST)
    weighted = (precisions.astype(jnp.float32)[:, None, :] * projected).astype(jnp.bfloat16)
    return jnp.einsum('ton,tco->tcn', wide_tiles, weighted.astype(jnp.float32), precision=HIGHEST)

def reference(x_cols, q_tiles, q_cols, halo_ids, a_tiles, obs_prec, tile_owner, tile_sub):
    blocks = x_cols.reshape(COLS, ROWBLOCKS, TB).transpose(1, 0, 2)
    sources = window_blocks(q_cols, halo_ids).reshape(PARTITIONS, RB_DEV * NB)
    q_grouped = q_tiles.reshape(PARTITIONS, RB_DEV * NB, TB, TB)

    def prior_part(paired):
        q_block, block_ids = paired
        x_blocks = blocks[block_ids].astype(jnp.float32)
        partial_value = jnp.einsum('kij,kcj->kci', q_block.astype(jnp.float32), x_blocks, precision=HIGHEST)
        return partial_value.reshape(RB_DEV, NB, COLS, TB).sum(axis=1)
    prior = lax.map(prior_part, (q_grouped, sources)).reshape(ROWBLOCKS, COLS, TB)
    targets = (tile_owner[:, 0] * RB_DEV + tile_sub).astype(jnp.int32).reshape(PARTITIONS, OT_DEV)

    def add_obs(running, paired):
        obs_tiles, precisions, block_ids = paired
        contrib = tile_terms(obs_tiles, precisions, blocks[block_ids])
        return (running.at[block_ids].add(contrib), None)
    start = jnp.zeros((ROWBLOCKS, COLS, TB), jnp.float32)
    observed, _ = lax.scan(add_obs, start, (a_tiles.reshape(PARTITIONS, OT_DEV, TB, TB), obs_prec.reshape(PARTITIONS, OT_DEV, TB), targets))
    combined = prior + observed
    product = combined.transpose(1, 0, 2).reshape(COLS, NODES)
    gram = jnp.dot(x_cols.astype(jnp.float32), product.T, precision=HIGHEST) / math.sqrt(NODES)
    return (product, gram)
```

```python
import functools
import math

import jax
import jax.numpy as jnp
from jax import lax
from jax.experimental import pallas as pl
from jax.experimental.pallas import tpu as pltpu
from jax.sharding import Mesh
from jax.sharding import PartitionSpec as P

LOGICAL = pl.DeviceIdType.MESH
Z, X, C, Y = 16, 4, 2, 4
PLANE = X * C
PARTS = Z * PLANE
TB = 128
COLS = 8
RB = 8
NB = 5
TILES = 64
SLOTS = 2 * Z
F32 = jnp.float32
BF16 = jnp.bfloat16
NT = (((1,), (1,)), ((), ()))
NN = (((1,), (0,)), ((), ()))


def kernel(
    x_ref, qc_ref, halo_ref, prec_ref, owner_ref, sub_ref, q_hbm, a_hbm,
    y_ref, g_ref,
    q_v, a_v, win, share, zx, xy, req, meta, req_s, meta_s, stage, xs, cb, stage2, rc, dn, zr, acc, g1, g2, gp, prec, mine,
    loc_sem, s_z, r_z, s_q, r_q, s_y, r_y, s_h, r_h, s_p, r_p, s_c, r_c, s_d, r_d, s_g1, r_g1, s_g2, r_g2,
):
    z, x, c, y = (lax.axis_index(n) for n in ("z", "x", "core", "col"))
    mq = x * C + c
    me = z * PLANE + mq

    def at_z(d):
        return {"z": lax.rem(z + d, Z)}

    def plane_peer(k):
        px, pc = lax.rem(x + k // C, X), lax.rem(c + k % C, C)
        return {"x": px, "core": pc}, px * C + pc

    def at_part(d):
        p = lax.rem(me + d + PARTS, PARTS)
        return {"z": p // PLANE, "x": lax.rem(p // C, X), "core": lax.rem(p, C)}

    def at_y(d):
        return {"col": lax.rem(y + d, Y)}

    def send(src, dst, ss, rs, where):
        return pltpu.make_async_remote_copy(
            src_ref=src, dst_ref=dst, send_sem=ss, recv_sem=rs, device_id=where, device_id_type=LOGICAL
        )

    barrier = pltpu.get_barrier_semaphore()
    halo_steps = (2, 1, -1, -2)
    others = [at_z(d) for d in range(1, Z)] + [plane_peer(k)[0] for k in range(1, PLANE)]
    others += [at_part(d) for d in halo_steps] + [at_y(d) for d in range(1, Y)]
    for other in others:
        pl.semaphore_signal(barrier, inc=1, device_id=other, device_id_type=LOGICAL)

    a_in = pltpu.make_async_copy(a_hbm, a_v, loc_sem.at[0])
    q_in = pltpu.make_async_copy(q_hbm, q_v, loc_sem.at[1])
    q_in.start()
    a_in.start()

    for r in range(RB):
        block = x_ref[:, r * TB:(r + 1) * TB]
        win[r] = block
        mine[r] = block
        zx[z, r] = block
    xy[y] = x_ref[...]
    for h in range(2):
        share[h] = mine[halo_ref[0, h]]

    prec[...] = prec_ref[...].astype(F32)
    shape = (TILES, TB)
    lane = lax.broadcasted_iota(jnp.int32, shape, 1)
    row = lax.broadcasted_iota(jnp.int32, shape, 0)
    eye = lane == row
    own_b = jnp.broadcast_to(owner_ref[...], shape)
    own_r = jnp.sum(jnp.where(eye, own_b, 0), axis=0, keepdims=True)
    sub_b = jnp.broadcast_to(jnp.sum(jnp.where(eye, sub_ref[...], 0), axis=1, keepdims=True), shape)
    same = own_b == own_r
    j_b = jnp.broadcast_to(
        jnp.sum(jnp.where(same & (lane < row), 1, 0), axis=1, keepdims=True), shape)
    j_r = jnp.sum(jnp.where(same & (row < lane), 1, 0), axis=0, keepdims=True)
    col_b = jnp.bitwise_and(own_b, PLANE - 1)
    key_b = jnp.right_shift(own_b, 3) * 2 + j_b
    for q in range(PLANE):
        hit = (col_b == q) & (key_b == lane)
        wanted = jnp.sum(jnp.where(hit, sub_b + 1, 0), axis=0, keepdims=True) - 1
        meta[q:q + 1] = wanted
        req[mq, q:q + 1] = wanted
        meta[PLANE + q:PLANE + q + 1] = jnp.sum(jnp.where(hit, row - TILES, 0), axis=0, keepdims=True) + TILES
    slot_r = jnp.bitwise_and(own_r, PLANE - 1) * SLOTS + jnp.right_shift(own_r, 3) * 2 + j_r
    meta[2 * PLANE:] = jnp.broadcast_to(slot_r, (8, TB))

    pl.semaphore_wait(barrier, len(others))

    def z_copy(d):
        return send(zx.at[z], zx.at[z], s_z.at[d], r_z.at[d], at_z(d))

    far_first = sorted(range(1, Z), key=lambda d: -min(d, Z - d))
    for d in far_first:
        z_copy(d).start()
    ask = [send(req.at[mq], req.at[mq], s_q.at[k], r_q.at[k], plane_peer(k)[0]) for k in range(1, PLANE)]
    for copy in ask:
        copy.start()
    halos = [
        send(share, win.at[pl.ds(RB + 2 * m, 2)], s_h.at[m], r_h.at[m], at_part(d))
        for m, d in enumerate(halo_steps)
    ]
    for copy in halos:
        copy.start()
    probes = [send(xy.at[y], xy.at[y], s_y.at[d], r_y.at[d], at_y(d)) for d in range(1, Y)]
    for copy in probes:
        copy.start()

    for copy in ask:
        copy.wait()
    to_req = pltpu.make_async_copy(req, req_s, loc_sem.at[2])
    to_meta = pltpu.make_async_copy(meta, meta_s, loc_sem.at[3])
    to_req.start()
    to_meta.start()

    for copy in halos:
        copy.wait()
    q_in.wait()

    def prior(r, carry):
        total = jnp.zeros((COLS, TB), F32)
        for k in range(NB):
            total += lax.dot_general(win[qc_ref[r, k]], q_v[r * NB + k], NT, preferred_element_type=F32)
        acc[r] = total
        return carry

    lax.fori_loop(0, RB, prior, 0)
    to_req.wait()
    to_meta.wait()
    a_in.wait()

    for d in far_first:
        z_copy(d).wait()

    def picked(k):
        _, q = plane_peer(k)

        def pick(s, carry):
            for j in range(2):
                sub = jnp.maximum(req_s[q, mq, 2 * s + j], 0)
                block = zx[s, sub]
                if k:
                    stage[k, 2 * s + j] = block
                else:
                    xs[mq * SLOTS + 2 * s + j] = block
            return carry

        lax.fori_loop(0, Z, pick, 0, unroll=4)

    gives = []
    for k in [6, 7, 2, 3, 4, 5, 1, 0]:
        picked(k)
        if k:
            copy = send(
                stage.at[k], xs.at[pl.ds(mq * SLOTS, SLOTS)], s_p.at[k], r_p.at[k], plane_peer(k)[0])
            copy.start()
            gives.append(copy)
    for copy in gives:
        copy.wait()

    def term(t, carry):
        tile = a_v[t]
        projected = lax.dot_general(xs[meta_s[2 * PLANE, t]], tile, NT, preferred_element_type=F32)
        weighted = (prec[pl.ds(t, 1), :] * projected).astype(BF16)
        cb[t] = lax.dot_general(weighted, tile, NN, preferred_element_type=F32)
        return carry

    lax.fori_loop(0, TILES, term, 0, unroll=8)
    cb[TILES] = jnp.zeros((COLS, TB), F32)

    backs = []
    for k in [6, 7, 2, 3, 4, 5, 1, 0]:
        where, q = plane_peer(k)

        def place(s, carry, k=k, q=q):
            block = cb[meta_s[PLANE + q, s]]
            if k:
                stage2[k, s] = block
            else:
                rc[mq, s] = block
            return carry

        lax.fori_loop(0, SLOTS, place, 0, unroll=8)
        if k:
            copy = send(stage2.at[k], rc.at[mq], s_c.at[k], r_c.at[k], where)
            copy.start()
            backs.append(copy)
    for copy in backs:
        copy.wait()

    def d_copy(d):
        return send(dn.at[d], zr.at[d], s_d.at[d], r_d.at[d], at_z(d))

    def dense(d, carry):
        dest = lax.rem(z + d, Z)
        totals = [jnp.zeros((COLS, TB), F32) for _ in range(RB)]
        for q in range(PLANE):
            for j in range(2):
                sub = jnp.broadcast_to(req_s[q, mq, 2 * dest + j], (COLS, TB))
                block = rc[q, 2 * dest + j]
                totals = [total + jnp.where(sub == r, block, 0.0) for r, total in enumerate(totals)]
        for r in range(RB):
            dn[d, r] = totals[r]
        return carry

    def dense_out(d, carry):
        dense(d, carry)
        d_copy(d).start()
        return carry

    lax.fori_loop(1, Z, dense_out, 0)
    dense(0, 0)
    for r in range(RB):
        acc[r] += dn[0, r]

    def landed(d, carry):
        d_copy(d).wait()
        for r in range(RB):
            acc[r] += zr[d, r]
        return carry

    lax.fori_loop(1, Z, landed, 0)
    for copy in probes:
        copy.wait()

    part = jnp.zeros((COLS, COLS * Y), F32)
    for r in range(RB):
        total = acc[r]
        y_ref[:, r * TB:(r + 1) * TB] = total
        across = jnp.concatenate([xy[i, :, r * TB:(r + 1) * TB] for i in range(Y)], axis=0)
        part += lax.dot_general(
            total, across.astype(F32), NT, precision=lax.Precision.HIGHEST, preferred_element_type=F32)
    gp[...] = jnp.zeros((COLS, TB), F32)
    gp[:, :COLS * Y] = part
    firsts = [send(gp, g1.at[k], s_g1.at[k], r_g1.at[k], plane_peer(k)[0]) for k in range(1, PLANE)]
    for copy in firsts:
        copy.start()
    g1[0] = gp[...]
    for copy in firsts:
        copy.wait()
    g2[0] = jnp.sum(g1[...], axis=0)
    seconds = [send(g2.at[0], g2.at[d], s_g2.at[d], r_g2.at[d], at_z(d)) for d in range(1, Z)]
    for copy in seconds:
        copy.start()
    for copy in seconds:
        copy.wait()
    g_ref[...] = jnp.sum(g2[...], axis=0) * (1.0 / math.sqrt(RB * TB * PARTS))


def body(x_cols, q_tiles, q_cols, halo_ids, a_tiles, obs_prec, tile_owner, tile_sub):
    vmem = pl.BlockSpec(memory_space=pltpu.VMEM)
    smem = pl.BlockSpec(memory_space=pltpu.SMEM)
    hbm = pl.BlockSpec(memory_space=pl.ANY)
    dma = pltpu.SemaphoreType.DMA
    block = (COLS, TB)
    product, gram = pl.pallas_call(
        kernel,
        out_shape=(
            jax.ShapeDtypeStruct((COLS, RB * TB), F32),
            jax.ShapeDtypeStruct((COLS, TB), F32),
        ),
        in_specs=[vmem, smem, smem, vmem, vmem, vmem, hbm, hbm],
        out_specs=(vmem, vmem),
        scratch_shapes=[
            pltpu.VMEM((RB * NB, TB, TB), BF16),
            pltpu.VMEM((TILES, TB, TB), BF16),
            pltpu.VMEM((RB + 8, *block), BF16),
            pltpu.VMEM((2, *block), BF16),
            pltpu.VMEM((Z, RB, *block), BF16),
            pltpu.VMEM((Y, COLS, RB * TB), BF16),
            pltpu.VMEM((PLANE, PLANE, TB), jnp.int32),
            pltpu.VMEM((2 * PLANE + 8, TB), jnp.int32),
            pltpu.SMEM((PLANE, PLANE, TB), jnp.int32),
            pltpu.SMEM((2 * PLANE + 8, TB), jnp.int32),
            pltpu.VMEM((PLANE, SLOTS, *block), BF16),
            pltpu.VMEM((PLANE * SLOTS, *block), BF16),
            pltpu.VMEM((TILES + 1, *block), F32),
            pltpu.VMEM((PLANE, SLOTS, *block), F32),
            pltpu.VMEM((PLANE, SLOTS, *block), F32),
            pltpu.VMEM((Z, RB, *block), F32),
            pltpu.VMEM((Z, RB, *block), F32),
            pltpu.VMEM((RB, *block), F32),
            pltpu.VMEM((PLANE, *block), F32),
            pltpu.VMEM((Z, *block), F32),
            pltpu.VMEM(block, F32),
            pltpu.VMEM((TILES, TB), F32),
            pltpu.VMEM((RB, *block), BF16),
            dma((4,)),
            dma((Z,)), dma((Z,)),
            dma((PLANE,)), dma((PLANE,)),
            dma((Y,)), dma((Y,)),
            dma((4,)), dma((4,)),
            dma((PLANE,)), dma((PLANE,)),
            dma((PLANE,)), dma((PLANE,)),
            dma((Z,)), dma((Z,)),
            dma((PLANE,)), dma((PLANE,)),
            dma((Z,)), dma((Z,)),
        ],
        compiler_params=pltpu.CompilerParams(
            collective_id=0, has_side_effects=True, vmem_limit_bytes=40 * 2**20),
        name="exchange",
    )(x_cols, q_cols, halo_ids, obs_prec, tile_owner, jnp.pad(tile_sub, (0, TB - TILES)).reshape(1, TB), q_tiles, a_tiles)
    return product, gram[:, :COLS * Y].T


def solution(mesh):
    torus = Mesh(mesh.devices.reshape(Z, X, C, Y), ("z", "x", "core", "col"))
    parts = ("z", "x", "core")
    in_specs = (
        P("col", parts),
        P(parts, None, None),
        P(parts, None),
        P(parts, None),
        P(parts, None, None),
        P(parts, None),
        P(parts, None),
        P(parts),
    )
    out_specs = (P("col", parts), P(None, "col"))
    return jax.shard_map(body, mesh=torus, in_specs=in_specs, out_specs=out_specs, check_vma=False)
```

```python
import math

import jax
import jax.numpy as jnp
from jax import lax
from jax.experimental import pallas as pl
from jax.experimental.pallas import tpu as pltpu
from jax.sharding import Mesh
from jax.sharding import PartitionSpec as P

LOGICAL = pl.DeviceIdType.MESH
Z, X, C, Y = 16, 4, 2, 4
PLANE = X * C
PARTS = Z * PLANE
TB = 128
COLS = 8
RB = 8
NB = 5
TILES = 64
SLOTS = 2 * Z
F32 = jnp.float32
BF16 = jnp.bfloat16
GROUP = 8
Z_PLAN = [(0, 5, None), (0, -5, None), (0, 1, None), (0, -1, None), (0, 2, None), (0, -2, None)]
Z_OWN = len(Z_PLAN)
Z_PLAN += [(-5, 3, 0), (-5, 2, None), (-5, -2, None), (-5, 1, None), (-5, -1, None)]
Z_PLAN += [(5, -3, 1), (5, 2, None), (5, -2, None), (5, 1, None), (5, -1, None)]
N_PLAN = [(8, -3, 0), (13, 2, None), (9, -2, None), (12, 1, None), (10, -1, None)]
N_PLAN += [(8, 3, 1), (7, 2, None), (3, -2, None), (6, 1, None), (4, -1, None)]
NT = (((1,), (1,)), ((), ()))
NN = (((1,), (0,)), ((), ()))


def kernel(
    x_hbm, qc_hbm, halo_hbm, prec_hbm, owner_hbm, sub_hbm, q_hbm, a_hbm,
    y_ref, g_ref,
    x_v, qc_s, halo_s, prec_in, own_v, sub_v,
    q_v, a_v, win, mine, share, zx, xy, req, meta, req_s, meta_s, stage, xs, cb, stage2, rc, dn, near, csum, direct,
    far, acc, g1, g2, gp, prec, pb, wb, pg,
    loc_sem, s_z, r_z, s_q, r_q, s_y, r_y, s_h, r_h, s_p, r_p, s_c, r_c, s_n, r_n, s_d, r_d, s_f, r_f, s_j, r_j,
    s_g1, r_g1, s_g2, r_g2,
):
    z, x, c, y = (lax.axis_index(n) for n in ("z", "x", "core", "col"))
    mq = x * C + c
    me = z * PLANE + mq

    def round_z(d):
        return lax.rem(z + d + Z, Z)

    def at_z(d):
        return {"z": round_z(d)}

    def plane_peer(k):
        px, pc = lax.rem(x + k // C, X), lax.rem(c + k % C, C)
        return {"x": px, "core": pc}, px * C + pc

    def at_part(d):
        p = lax.rem(me + d + PARTS, PARTS)
        return {"z": p // PLANE, "x": lax.rem(p // C, X), "core": lax.rem(p, C)}

    def at_y(d):
        return {"col": lax.rem(y + d, Y)}

    def send(src, dst, sems, i, where):
        return pltpu.make_async_remote_copy(
            src_ref=src, dst_ref=dst, send_sem=sems[0].at[i], recv_sem=sems[1].at[i],
            device_id=where, device_id_type=LOGICAL,
        )

    def start(copies):
        for copy in copies:
            copy.start()
        return copies

    def finish(copies):
        for copy in copies:
            copy.wait()

    loads = [
        pltpu.make_async_copy(src, dst, loc_sem.at[i])
        for i, (src, dst) in enumerate((
            (x_hbm, x_v), (halo_hbm, halo_s), (owner_hbm, own_v), (sub_hbm, sub_v), (prec_hbm, prec_in),
            (qc_hbm, qc_s), (q_hbm, q_v), (a_hbm, a_v),
        ))
    ]
    start(loads)
    x_in, halo_in, own_in, sub_in, prec_load, qc_in, q_in, a_in = loads

    barrier = pltpu.get_barrier_semaphore()
    halo_steps = (2, 1, -1, -2)
    others = [at_z(d) for d in range(1, Z)] + [plane_peer(k)[0] for k in range(1, PLANE)]
    others += [at_part(d) for d in halo_steps] + [at_y(d) for d in range(1, Y)]
    for other in others:
        pl.semaphore_signal(barrier, inc=1, device_id=other, device_id_type=LOGICAL)

    x_in.wait()
    halo_in.wait()
    for r in range(RB):
        block = x_v[:, r * TB:(r + 1) * TB]
        win[r] = block
        mine[r] = block
        zx[z, r] = block
    xy[y] = x_v[...]
    for h in range(2):
        share[h] = mine[halo_s[0, h]]

    def z_copy(i):
        hold, step, half = Z_PLAN[i]
        origin = round_z(hold)
        part = zx.at[origin] if half is None else zx.at[origin, pl.ds(half * (RB // 2), RB // 2)]
        return send(part, part, (s_z, r_z), i, at_z(step))

    z_copies = [z_copy(i) for i in range(len(Z_PLAN))]

    pl.semaphore_wait(barrier, len(others))

    start(z_copies[:Z_OWN])
    halos = start([
        send(share, win.at[pl.ds(RB + 2 * m, 2)], (s_h, r_h), m, at_part(d))
        for m, d in enumerate(halo_steps)
    ])
    probes = start([send(x_v, xy.at[y], (s_y, r_y), d, at_y(d)) for d in range(1, Y)])

    own_in.wait()
    sub_in.wait()
    prec_load.wait()
    prec[...] = prec_in[...].astype(F32)
    shape = (TILES, TB)
    lane = lax.broadcasted_iota(jnp.int32, shape, 1)
    row = lax.broadcasted_iota(jnp.int32, shape, 0)
    eye = lane == row
    fill = jnp.full((1, TB - TILES), -1, jnp.int32)
    own_r = jnp.concatenate([own_v[...], fill], axis=1)
    sub_r = jnp.concatenate([sub_v[...], fill], axis=1)
    own_b = jnp.broadcast_to(jnp.sum(jnp.where(eye, own_r, 0), axis=1, keepdims=True), shape)
    sub_b = jnp.broadcast_to(jnp.sum(jnp.where(eye, sub_r, 0), axis=1, keepdims=True), shape)
    same = own_b == own_r
    j_b = jnp.broadcast_to(
        jnp.sum(jnp.where(same & (lane < row), 1, 0), axis=1, keepdims=True), shape)
    j_r = jnp.sum(jnp.where(same & (row < lane), 1, 0), axis=0, keepdims=True)
    col_b = jnp.bitwise_and(own_b, PLANE - 1)
    key_b = jnp.right_shift(own_b, 3) * 2 + j_b
    for q in range(PLANE):
        hit = (col_b == q) & (key_b == lane)
        wanted = jnp.sum(jnp.where(hit, sub_b + 1, 0), axis=0, keepdims=True) - 1
        req[mq, q:q + 1] = wanted
        meta[PLANE + q:PLANE + q + 1] = jnp.sum(jnp.where(hit, row - TILES, 0), axis=0, keepdims=True) + TILES
    slot_r = jnp.bitwise_and(own_r, PLANE - 1) * SLOTS + jnp.right_shift(own_r, 3) * 2 + j_r
    meta[:PLANE] = jnp.broadcast_to(slot_r, (8, TB))
    to_meta = pltpu.make_async_copy(meta, meta_s, loc_sem.at[8])
    to_meta.start()
    asks = start([send(req.at[mq], req.at[mq], (s_q, r_q), k, plane_peer(k)[0]) for k in range(1, PLANE)])

    for i in range(2):
        z_copies[i].wait_recv()
        start(z_copies[Z_OWN + 5 * i:Z_OWN + 5 * i + 5])

    finish(asks)
    to_req = pltpu.make_async_copy(req, req_s, loc_sem.at[9])
    to_req.start()

    finish(halos)
    qc_in.wait()
    q_in.wait()

    def prior(r, carry):
        total = jnp.zeros((COLS, TB), F32)
        for k in range(NB):
            total += lax.dot_general(win[qc_s[r, k]], q_v[r * NB + k], NT, preferred_element_type=F32)
        acc[r] = total
        return carry

    lax.fori_loop(0, RB, prior, 0, unroll=2)
    to_req.wait()
    to_meta.wait()
    a_in.wait()

    for i, copy in enumerate(z_copies):
        copy.wait_send()
        if i >= 2:
            copy.wait_recv()

    order = [6, 7, 2, 3, 4, 5, 1, 0]
    gives = []
    for k in order:
        where, q = plane_peer(k)

        def pick(s, carry, k=k, q=q):
            for j in range(2):
                block = zx[s, jnp.maximum(req_s[q, mq, 2 * s + j], 0)]
                if k:
                    stage[k, 2 * s + j] = block
                else:
                    xs[mq * SLOTS + 2 * s + j] = block
            return carry

        lax.fori_loop(0, Z, pick, 0, unroll=8)
        if k:
            gives += start([send(stage.at[k], xs.at[pl.ds(mq * SLOTS, SLOTS)], (s_p, r_p), k, where)])
    finish(gives)

    def terms(group, carry):
        base = pl.multiple_of(group * GROUP, GROUP)
        scales = prec[pl.ds(base, GROUP), :]
        tiles, projected, weighted = [], [], []
        for i in range(0, GROUP, 2):
            tile = a_v[pl.ds(base + i, 2)].reshape(2 * TB, TB)
            pair = jnp.concatenate([xs[meta_s[0, base + i]], xs[meta_s[0, base + i + 1]]], axis=0)
            tiles.append(tile)
            projected.append(lax.dot_general(pair, tile, NT, preferred_element_type=F32))
        zero = jnp.zeros((COLS, TB), F32)
        for i in range(0, GROUP, 2):
            both = projected[i // 2]
            top, low = both[:COLS, :TB], both[COLS:, TB:]
            top_w, low_w = scales[i:i + 1] * top, scales[i + 1:i + 2] * low
            block = jnp.concatenate([
                jnp.concatenate([top_w, zero], axis=1), jnp.concatenate([zero, low_w], axis=1)], axis=0)
            weighted.append(block.astype(BF16))
            for h, (p, w) in enumerate(((top, top_w), (low, low_w))):
                lanes = pl.ds(pl.multiple_of((base + i + h) * TB, TB), TB)
                pb[:, lanes] = p.astype(BF16)
                wb[:, lanes] = w.astype(BF16)
        for i in range(0, GROUP, 2):
            both = lax.dot_general(weighted[i // 2], tiles[i // 2], NN, preferred_element_type=F32)
            cb[base + i] = both[:COLS]
            cb[base + i + 1] = both[COLS:]
        return carry

    lax.fori_loop(0, TILES // GROUP, terms, 0)
    cb[TILES] = jnp.zeros((COLS, TB), F32)

    backs = []
    for k in order:
        where, q = plane_peer(k)

        def place(s, carry, k=k, q=q):
            block = cb[meta_s[PLANE + q, s]]
            if k:
                stage2[k, s] = block
            else:
                rc[mq, s] = block
            return carry

        lax.fori_loop(0, SLOTS, place, 0, unroll=8)
        if k:
            backs += start([send(stage2.at[k], rc.at[mq], (s_c, r_c), k, where)])

    turns = start([send(pb, pg.at[y], (s_j, r_j), d, at_y(d)) for d in range(1, Y)])
    pg[y] = pb[...]
    finish(probes)
    part = jnp.zeros((COLS, COLS * Y), F32)
    for r in range(RB):
        across = jnp.concatenate([xy[i, :, r * TB:(r + 1) * TB] for i in range(Y)], axis=0)
        part += lax.dot_general(
            acc[r], across.astype(F32), NT, precision=lax.Precision.HIGHEST, preferred_element_type=F32)
    finish(turns)

    def gram_part(i, part):
        lanes = pl.ds(pl.multiple_of(i * 1024, 1024), 1024)
        across = jnp.concatenate([pg[j, :, lanes] for j in range(Y)], axis=0)
        return part + lax.dot_general(wb[:, lanes], across, NT, preferred_element_type=F32)

    part = lax.fori_loop(0, TILES * TB // 1024, gram_part, part)
    gp[...] = jnp.zeros((COLS, TB), F32)
    gp[:, :COLS * Y] = part
    firsts = start([send(gp, g1.at[k], (s_g1, r_g1), k, plane_peer(k)[0]) for k in range(1, PLANE)])
    g1[0] = gp[...]
    finish(backs)

    def dense(i, carry):
        d = lax.rem(i, Z)
        dest = lax.rem(z + d, Z)
        totals = [jnp.zeros((COLS, TB), F32) for _ in range(RB)]
        for q in range(PLANE):
            for j in range(2):
                sub = jnp.broadcast_to(req_s[q, mq, 2 * dest + j], (COLS, TB))
                block = rc[q, 2 * dest + j]
                totals = [total + jnp.where(sub == r, block, 0.0) for r, total in enumerate(totals)]
        for r in range(RB):
            dn[d, r] = totals[r]
        return carry

    lax.fori_loop(3, 14, dense, 0)
    nears = []
    for i, (d, step, half) in enumerate(N_PLAN):
        if half is None:
            src, dst = dn.at[d], near.at[i]
        else:
            rows = pl.ds(half * (RB // 2), RB // 2)
            src, dst = dn.at[d, rows], near.at[i, rows]
        nears += start([send(src, dst, (s_n, r_n), i, at_z(step))])
    lax.fori_loop(14, 19, dense, 0)
    directs = start([send(dn.at[d % Z], direct.at[i], (s_d, r_d), i, at_z(d)) for i, d in enumerate((1, -1, 2, -2))])
    finish(firsts)
    g2[0] = jnp.sum(g1[...], axis=0)
    seconds = start([send(g2.at[0], g2.at[d], (s_g2, r_g2), d, at_z(d)) for d in range(1, Z)])

    finish(nears)
    fars = []
    for g, d in enumerate((-5, 5)):
        for r in range(RB):
            total = dn[d % Z, r]
            for i in range(4):
                total += near[5 * g + 1 + i, r]
            if r // (RB // 2) == g:
                total += near[5 * g, r]
            csum[g, r] = total
        fars += start([send(csum.at[g], far.at[g], (s_f, r_f), g, at_z(d))])
    finish(directs)
    for r in range(RB):
        acc[r] += (dn[0, r] + direct[0, r]) + (direct[1, r] + direct[2, r]) + direct[3, r]
    finish(seconds)
    g_ref[...] = (jnp.sum(g2[...], axis=0) * (1.0 / math.sqrt(RB * TB * PARTS)))[:, :COLS * Y]
    finish(fars)
    for r in range(RB):
        y_ref[:, r * TB:(r + 1) * TB] = acc[r] + (far[0, r] + far[1, r])


def body(x_cols, q_tiles, q_cols, halo_ids, a_tiles, obs_prec, tile_owner, tile_sub):
    vmem = pl.BlockSpec(memory_space=pltpu.VMEM)
    hbm = pl.BlockSpec(memory_space=pl.ANY)
    block = (COLS, TB)

    def pair(n):
        return [pltpu.SemaphoreType.DMA((n,))] * 2

    product, gram = pl.pallas_call(
        kernel,
        out_shape=(
            jax.ShapeDtypeStruct((COLS, RB * TB), F32),
            jax.ShapeDtypeStruct((COLS, COLS * Y), F32),
        ),
        in_specs=[hbm] * 8,
        out_specs=(vmem, vmem),
        scratch_shapes=[
            pltpu.VMEM((COLS, RB * TB), BF16),
            pltpu.SMEM((RB, NB), jnp.int32),
            pltpu.SMEM((1, 2), jnp.int32),
            pltpu.VMEM((TILES, TB), BF16),
            pltpu.VMEM((1, TILES), jnp.int32),
            pltpu.VMEM((1, TILES), jnp.int32),
            pltpu.VMEM((RB * NB, TB, TB), BF16),
            pltpu.VMEM((TILES, TB, TB), BF16),
            pltpu.VMEM((RB + 8, *block), BF16),
            pltpu.VMEM((RB, *block), BF16),
            pltpu.VMEM((2, *block), BF16),
            pltpu.VMEM((Z, RB, *block), BF16),
            pltpu.VMEM((Y, COLS, RB * TB), BF16),
            pltpu.VMEM((PLANE, PLANE, TB), jnp.int32),
            pltpu.VMEM((2 * PLANE, TB), jnp.int32),
            pltpu.SMEM((PLANE, PLANE, TB), jnp.int32),
            pltpu.SMEM((2 * PLANE, TB), jnp.int32),
            pltpu.VMEM((PLANE, SLOTS, *block), BF16),
            pltpu.VMEM((PLANE * SLOTS, *block), BF16),
            pltpu.VMEM((TILES + 1, *block), F32),
            pltpu.VMEM((PLANE, SLOTS, *block), F32),
            pltpu.VMEM((PLANE, SLOTS, *block), F32),
            pltpu.VMEM((Z, RB, *block), F32),
            pltpu.VMEM((len(N_PLAN), RB, *block), F32),
            pltpu.VMEM((2, RB, *block), F32),
            pltpu.VMEM((4, RB, *block), F32),
            pltpu.VMEM((2, RB, *block), F32),
            pltpu.VMEM((RB, *block), F32),
            pltpu.VMEM((PLANE, *block), F32),
            pltpu.VMEM((Z, *block), F32),
            pltpu.VMEM(block, F32),
            pltpu.VMEM((TILES, TB), F32),
            pltpu.VMEM((COLS, TILES * TB), BF16),
            pltpu.VMEM((COLS, TILES * TB), BF16),
            pltpu.VMEM((Y, COLS, TILES * TB), BF16),
            pltpu.SemaphoreType.DMA((10,)),
            *pair(len(Z_PLAN)),
            *pair(PLANE),
            *pair(Y),
            *pair(4),
            *pair(PLANE),
            *pair(PLANE),
            *pair(len(N_PLAN)),
            *pair(4),
            *pair(2),
            *pair(Y),
            *pair(PLANE),
            *pair(Z),
        ],
        compiler_params=pltpu.CompilerParams(
            collective_id=0, has_side_effects=True, vmem_limit_bytes=60 * 2**20),
        name="exchange",
    )(
        x_cols, q_cols, halo_ids, obs_prec, tile_owner.reshape(1, TILES), tile_sub.reshape(1, TILES),
        q_tiles, a_tiles,
    )
    return product, gram.T


def solution(mesh):
    torus = Mesh(mesh.devices.reshape(Z, X, C, Y), ("z", "x", "core", "col"))
    parts = ("z", "x", "core")
    in_specs = (
        P("col", parts),
        P(parts, None, None),
        P(parts, None),
        P(parts, None),
        P(parts, None, None),
        P(parts, None),
        P(parts, None),
        P(parts),
    )
    out_specs = (P("col", parts), P(None, "col"))
    return jax.shard_map(body, mesh=torus, in_specs=in_specs, out_specs=out_specs, check_vma=False)
```

```python
import math

import jax
import jax.numpy as jnp
from jax import lax
from jax.experimental import pallas as pl
from jax.experimental.pallas import tpu as pltpu
from jax.sharding import Mesh
from jax.sharding import PartitionSpec as P

LOGICAL = pl.DeviceIdType.MESH
Z, X, C, Y = 16, 4, 2, 4
PLANE = X * C
PARTS = Z * PLANE
TB = 128
COLS = 8
RB = 8
NB = 5
TILES = 64
SLOTS = 2 * Z
F32 = jnp.float32
BF16 = jnp.bfloat16
GROUP = 8
Z_PLAN = [(0, 5, None), (0, -5, None), (0, 1, None), (0, -1, None), (0, 2, None), (0, -2, None)]
Z_OWN = len(Z_PLAN)
Z_PLAN += [(-5, 3, 0), (-5, 2, None), (-5, -2, None), (-5, 1, None), (-5, -1, None)]
Z_PLAN += [(5, -3, 1), (5, 2, None), (5, -2, None), (5, 1, None), (5, -1, None)]
ORDER = (0, 1, 15, 2, 14, 5, 11, 3, 4, 6, 7, 8, 9, 10, 12, 13)
FIRST = 7
WAVES = ((0, FIRST), (FIRST, Z))
N_PLAN = [(8, -3, 0), (13, 2, None), (9, -2, None), (12, 1, None), (10, -1, None)]
N_PLAN += [(8, 3, 1), (7, 2, None), (3, -2, None), (6, 1, None), (4, -1, None)]
NT = (((1,), (1,)), ((), ()))
NN = (((1,), (0,)), ((), ()))


def kernel(
    x_hbm, qc_hbm, halo_hbm, prec_hbm, owner_hbm, sub_hbm, q_hbm, a_hbm,
    y_ref, g_ref,
    x_v, qc_s, halo_s, prec_in, own_v, sub_v,
    q_v, a_v, win, mine, share, zx, zy, xy, req, meta, req_s, meta_s, stage, xs, cb, stage2, rc, dn, near, csum, direct,
    far, acc, g1, g2, gp, prec, pb, wb, pg,
    loc_sem, s_z, r_z, s_q, r_q, s_y, r_y, s_h, r_h, s_p, r_p, s_c, r_c, s_n, r_n, s_d, r_d, s_f, r_f, s_j, r_j,
    s_g1, r_g1, s_g2, r_g2,
):
    z, x, c, y = (lax.axis_index(n) for n in ("z", "x", "core", "col"))
    mq = x * C + c
    me = z * PLANE + mq

    def round_z(d):
        return lax.rem(z + d + Z, Z)

    def at_z(d):
        return {"z": round_z(d)}

    def plane_peer(k):
        px, pc = lax.rem(x + k // C, X), lax.rem(c + k % C, C)
        return {"x": px, "core": pc}, px * C + pc

    def at_part(d):
        p = lax.rem(me + d + PARTS, PARTS)
        return {"z": p // PLANE, "x": lax.rem(p // C, X), "core": lax.rem(p, C)}

    def at_y(d):
        return {"col": lax.rem(y + d, Y)}

    def send(src, dst, sems, i, where):
        return pltpu.make_async_remote_copy(
            src_ref=src, dst_ref=dst, send_sem=sems[0].at[i], recv_sem=sems[1].at[i],
            device_id=where, device_id_type=LOGICAL,
        )

    def start(copies):
        for copy in copies:
            copy.start()
        return copies

    def finish(copies):
        for copy in copies:
            copy.wait()

    loads = [
        pltpu.make_async_copy(src, dst, loc_sem.at[i])
        for i, (src, dst) in enumerate((
            (x_hbm, x_v), (halo_hbm, halo_s), (owner_hbm, own_v), (sub_hbm, sub_v), (prec_hbm, prec_in),
            (qc_hbm, qc_s), (q_hbm, q_v), (a_hbm, a_v),
        ))
    ]
    start(loads)
    x_in, halo_in, own_in, sub_in, prec_load, qc_in, q_in, a_in = loads

    barrier = pltpu.get_barrier_semaphore()
    halo_steps = (2, 1, -1, -2)
    others = [at_z(d) for d in range(1, Z)] + [plane_peer(k)[0] for k in range(1, PLANE)]
    others += [at_part(d) for d in halo_steps] + [at_y(d) for d in range(1, Y)]
    for other in others:
        pl.semaphore_signal(barrier, inc=1, device_id=other, device_id_type=LOGICAL)

    x_in.wait()
    halo_in.wait()
    for r in range(RB):
        block = x_v[:, r * TB:(r + 1) * TB]
        win[r] = block
        mine[r] = block
        zx[0, r] = block
    xy[y] = x_v[...]
    for h in range(2):
        share[h] = mine[halo_s[0, h]]

    def chunk(d):
        i = ORDER.index(d % Z)
        return zx.at[i] if i < FIRST else zy.at[i - FIRST]

    def z_copy(i):
        hold, step, half = Z_PLAN[i]
        src, dst = chunk(hold), chunk(hold - step)
        if half is not None:
            rows = pl.ds(half * (RB // 2), RB // 2)
            src, dst = src.at[rows], dst.at[rows]
        return send(src, dst, (s_z, r_z), i, at_z(step))

    z_copies = [z_copy(i) for i in range(len(Z_PLAN))]

    pl.semaphore_wait(barrier, len(others))

    start(z_copies[:Z_OWN])
    halos = start([
        send(share, win.at[pl.ds(RB + 2 * m, 2)], (s_h, r_h), m, at_part(d))
        for m, d in enumerate(halo_steps)
    ])
    probes = start([send(x_v, xy.at[y], (s_y, r_y), d, at_y(d)) for d in range(1, Y)])

    own_in.wait()
    sub_in.wait()
    prec_load.wait()
    prec[...] = prec_in[...].astype(F32)
    shape = (TILES, TB)
    lane = lax.broadcasted_iota(jnp.int32, shape, 1)
    row = lax.broadcasted_iota(jnp.int32, shape, 0)
    eye = lane == row
    fill = jnp.full((1, TB - TILES), -1, jnp.int32)
    own_r = jnp.concatenate([own_v[...], fill], axis=1)
    sub_r = jnp.concatenate([sub_v[...], fill], axis=1)
    own_b = jnp.broadcast_to(jnp.sum(jnp.where(eye, own_r, 0), axis=1, keepdims=True), shape)
    sub_b = jnp.broadcast_to(jnp.sum(jnp.where(eye, sub_r, 0), axis=1, keepdims=True), shape)
    same = own_b == own_r
    j_b = jnp.broadcast_to(
        jnp.sum(jnp.where(same & (lane < row), 1, 0), axis=1, keepdims=True), shape)
    j_r = jnp.sum(jnp.where(same & (row < lane), 1, 0), axis=0, keepdims=True)
    col_b = jnp.bitwise_and(own_b, PLANE - 1)

    def place_of(owner):
        offset = jnp.bitwise_and(jnp.right_shift(owner, 3) - z, Z - 1)
        return sum(jnp.where(offset == d, 2 * i, 0) for i, d in enumerate(ORDER) if i)

    key_b = place_of(own_b) + j_b
    for q in range(PLANE):
        hit = (col_b == q) & (key_b == lane)
        wanted = jnp.sum(jnp.where(hit, sub_b + 1, 0), axis=0, keepdims=True) - 1
        req[mq, q:q + 1] = wanted
        meta[PLANE + q:PLANE + q + 1] = jnp.sum(jnp.where(hit, row - TILES, 0), axis=0, keepdims=True) + TILES
    slot_r = jnp.bitwise_and(own_r, PLANE - 1) * SLOTS + place_of(own_r) + j_r
    meta[:PLANE] = jnp.broadcast_to(slot_r, (8, TB))
    to_meta = pltpu.make_async_copy(meta, meta_s, loc_sem.at[8])
    to_meta.start()
    asks = start([send(req.at[mq], req.at[mq], (s_q, r_q), k, plane_peer(k)[0]) for k in range(1, PLANE)])

    for i in range(2):
        z_copies[i].wait_recv()
        start(z_copies[Z_OWN + 5 * i:Z_OWN + 5 * i + 5])

    finish(asks)
    to_req = pltpu.make_async_copy(req, req_s, loc_sem.at[9])
    to_req.start()
    for copy in z_copies[2:Z_OWN]:
        copy.wait_recv()
    to_req.wait()

    def give(wave, k):
        low, high = WAVES[wave]
        slots = pl.ds(2 * low, 2 * (high - low))
        return send(stage.at[k, slots], xs.at[mq, slots], (s_p.at[wave], r_p.at[wave]), k, plane_peer(k)[0])

    def pick(wave, k, dst):
        _, q = plane_peer(k)
        held, low = (zy, FIRST) if wave else (zx, 0)
        for i in range(*WAVES[wave]):
            for j in range(2):
                dst[2 * i + j] = held[i - low, jnp.maximum(req_s[q, mq, 2 * i + j], 0)]

    for wave in range(2):
        if wave:
            for copy in z_copies[Z_OWN:]:
                copy.wait_recv()

        def hand_out(i, carry, wave=wave):
            k = lax.rem(i + 3, PLANE - 1) + 1
            pick(wave, k, stage.at[k])
            give(wave, k).start()
            return carry

        lax.fori_loop(0, PLANE - 1, hand_out, 0)
        pick(wave, 0, xs.at[mq])
    to_meta.wait()
    a_in.wait()
    for copy in z_copies:
        copy.wait_send()
    for wave in range(2):
        finish([give(wave, k) for k in range(1, PLANE)])

    xs_flat = xs.reshape(PLANE * SLOTS, COLS, TB)

    def terms(group, carry):
        base = pl.multiple_of(group * GROUP, GROUP)
        scales = prec[pl.ds(base, GROUP), :]
        tiles, projected, weighted = [], [], []
        for i in range(0, GROUP, 2):
            tile = a_v[pl.ds(base + i, 2)].reshape(2 * TB, TB)
            pair = jnp.concatenate([xs_flat[meta_s[0, base + i]], xs_flat[meta_s[0, base + i + 1]]], axis=0)
            tiles.append(tile)
            projected.append(lax.dot_general(pair, tile, NT, preferred_element_type=F32))
        zero = jnp.zeros((COLS, TB), F32)
        for i in range(0, GROUP, 2):
            both = projected[i // 2]
            top, low = both[:COLS, :TB], both[COLS:, TB:]
            top_w, low_w = scales[i:i + 1] * top, scales[i + 1:i + 2] * low
            block = jnp.concatenate([
                jnp.concatenate([top_w, zero], axis=1), jnp.concatenate([zero, low_w], axis=1)], axis=0)
            weighted.append(block.astype(BF16))
            for h, (p, w) in enumerate(((top, top_w), (low, low_w))):
                lanes = pl.ds(pl.multiple_of((base + i + h) * TB, TB), TB)
                pb[:, lanes] = p.astype(BF16)
                wb[:, lanes] = w.astype(BF16)
        for i in range(0, GROUP, 2):
            both = lax.dot_general(weighted[i // 2], tiles[i // 2], NN, preferred_element_type=F32)
            cb[base + i] = both[:COLS]
            cb[base + i + 1] = both[COLS:]
        return carry

    lax.fori_loop(0, TILES // GROUP, terms, 0)
    cb[TILES] = jnp.zeros((COLS, TB), F32)
    turns = start([send(pb, pg.at[y], (s_j, r_j), d, at_y(d)) for d in range(1, Y)])

    def back(wave, k):
        low, high = WAVES[wave]
        slots = pl.ds(2 * low, 2 * (high - low))
        return send(stage2.at[k, slots], rc.at[mq, slots], (s_c.at[wave], r_c.at[wave]), k, plane_peer(k)[0])

    def place(wave, k, dst):
        _, q = plane_peer(k)
        for i in range(2 * WAVES[wave][0], 2 * WAVES[wave][1]):
            dst[i] = cb[meta_s[PLANE + q, i]]

    for wave in (1, 0):

        def hand_back(i, carry, wave=wave):
            k = lax.rem(i + 3, PLANE - 1) + 1
            place(wave, k, stage2.at[k])
            back(wave, k).start()
            return carry

        lax.fori_loop(0, PLANE - 1, hand_back, 0)
        place(wave, 0, rc.at[mq])

    pg[y] = pb[...]
    finish(halos)
    qc_in.wait()
    q_in.wait()

    def prior(r, carry):
        total = jnp.zeros((COLS, TB), F32)
        for k in range(NB):
            total += lax.dot_general(win[qc_s[r, k]], q_v[r * NB + k], NT, preferred_element_type=F32)
        acc[r] = total
        return carry

    lax.fori_loop(0, RB, prior, 0, unroll=4)
    finish(probes)
    part = jnp.zeros((COLS, COLS * Y), F32)
    for r in range(RB):
        across = jnp.concatenate([xy[i, :, r * TB:(r + 1) * TB] for i in range(Y)], axis=0)
        part += lax.dot_general(
            acc[r], across.astype(F32), NT, precision=lax.Precision.HIGHEST, preferred_element_type=F32)
    finish(turns)

    def gram_part(i, part):
        lanes = pl.ds(pl.multiple_of(i * 1024, 1024), 1024)
        across = jnp.concatenate([pg[j, :, lanes] for j in range(Y)], axis=0)
        return part + lax.dot_general(wb[:, lanes], across, NT, preferred_element_type=F32)

    part = lax.fori_loop(0, TILES * TB // 1024, gram_part, part)
    gp[...] = jnp.concatenate([part[2 * i:2 * i + 2] for i in range(COLS // 2)], axis=1)
    firsts = start([send(gp, g1.at[k], (s_g1, r_g1), k, plane_peer(k)[0]) for k in range(1, PLANE)])
    g1[0] = gp[...]

    def dense(i, carry):
        totals = [jnp.zeros((COLS, TB), F32) for _ in range(RB)]
        for q in range(PLANE):
            for j in range(2):
                sub = jnp.broadcast_to(req_s[q, mq, 2 * i + j], (COLS, TB))
                block = rc[q, 2 * i + j]
                totals = [total + jnp.where(sub == r, block, 0.0) for r, total in enumerate(totals)]
        for r in range(RB):
            dn[i, r] = totals[r]
        return carry

    def sums_for(d):
        return dn.at[ORDER.index(d % Z)]

    finish([back(1, k) for k in range(1, PLANE)])
    lax.fori_loop(*WAVES[1], dense, 0)
    nears = []
    for i, (d, step, half) in enumerate(N_PLAN):
        src, dst = sums_for(d), near.at[i]
        if half is not None:
            rows = pl.ds(half * (RB // 2), RB // 2)
            src, dst = src.at[rows], dst.at[rows]
        nears += start([send(src, dst, (s_n, r_n), i, at_z(step))])
    finish(firsts)
    g2[0] = jnp.sum(g1[...], axis=0)
    seconds = start([send(g2.at[0], g2.at[d], (s_g2, r_g2), d, at_z(d)) for d in range(1, Z)])
    finish([back(0, k) for k in range(1, PLANE)])
    lax.fori_loop(*WAVES[0], dense, 0)
    directs = start([send(sums_for(d), direct.at[i], (s_d, r_d), i, at_z(d)) for i, d in enumerate((1, -1, 2, -2))])
    finish(nears)
    fars = []
    for g, d in enumerate((-5, 5)):
        for r in range(RB):
            total = sums_for(d)[r]
            for i in range(4):
                total += near[5 * g + 1 + i, r]
            if r // (RB // 2) == g:
                total += near[5 * g, r]
            csum[g, r] = total
        fars += start([send(csum.at[g], far.at[g], (s_f, r_f), g, at_z(d))])
    finish(directs)
    for r in range(RB):
        acc[r] += (dn[0, r] + direct[0, r]) + (direct[1, r] + direct[2, r]) + direct[3, r]
    finish(seconds)
    total = jnp.sum(g2[...], axis=0) * (1.0 / math.sqrt(RB * TB * PARTS))
    width = COLS * Y
    g_ref[...] = jnp.concatenate([total[:, i * width:(i + 1) * width] for i in range(COLS // 2)], axis=0)
    finish(fars)
    for r in range(RB):
        y_ref[:, r * TB:(r + 1) * TB] = acc[r] + (far[0, r] + far[1, r])


def body(x_cols, q_tiles, q_cols, halo_ids, a_tiles, obs_prec, tile_owner, tile_sub):
    vmem = pl.BlockSpec(memory_space=pltpu.VMEM)
    hbm = pl.BlockSpec(memory_space=pl.ANY)
    block = (COLS, TB)

    def pair(*shape):
        return [pltpu.SemaphoreType.DMA(shape)] * 2

    product, gram = pl.pallas_call(
        kernel,
        out_shape=(
            jax.ShapeDtypeStruct((COLS, RB * TB), F32),
            jax.ShapeDtypeStruct((COLS, COLS * Y), F32),
        ),
        in_specs=[hbm] * 8,
        out_specs=(vmem, vmem),
        scratch_shapes=[
            pltpu.VMEM((COLS, RB * TB), BF16),
            pltpu.SMEM((RB, NB), jnp.int32),
            pltpu.SMEM((1, 2), jnp.int32),
            pltpu.VMEM((TILES, TB), BF16),
            pltpu.VMEM((1, TILES), jnp.int32),
            pltpu.VMEM((1, TILES), jnp.int32),
            pltpu.VMEM((RB * NB, TB, TB), BF16),
            pltpu.VMEM((TILES, TB, TB), BF16),
            pltpu.VMEM((RB + 8, *block), BF16),
            pltpu.VMEM((RB, *block), BF16),
            pltpu.VMEM((2, *block), BF16),
            pltpu.VMEM((FIRST, RB, *block), BF16),
            pltpu.VMEM((Z - FIRST, RB, *block), BF16),
            pltpu.VMEM((Y, COLS, RB * TB), BF16),
            pltpu.VMEM((PLANE, PLANE, TB), jnp.int32),
            pltpu.VMEM((2 * PLANE, TB), jnp.int32),
            pltpu.SMEM((PLANE, PLANE, TB), jnp.int32),
            pltpu.SMEM((2 * PLANE, TB), jnp.int32),
            pltpu.VMEM((PLANE, SLOTS, *block), BF16),
            pltpu.VMEM((PLANE, SLOTS, *block), BF16),
            pltpu.VMEM((TILES + 1, *block), F32),
            pltpu.VMEM((PLANE, SLOTS, *block), F32),
            pltpu.VMEM((PLANE, SLOTS, *block), F32),
            pltpu.VMEM((Z, RB, *block), F32),
            pltpu.VMEM((len(N_PLAN), RB, *block), F32),
            pltpu.VMEM((2, RB, *block), F32),
            pltpu.VMEM((4, RB, *block), F32),
            pltpu.VMEM((2, RB, *block), F32),
            pltpu.VMEM((RB, *block), F32),
            pltpu.VMEM((PLANE, 2, TB), F32),
            pltpu.VMEM((Z, 2, TB), F32),
            pltpu.VMEM((2, TB), F32),
            pltpu.VMEM((TILES, TB), F32),
            pltpu.VMEM((COLS, TILES * TB), BF16),
            pltpu.VMEM((COLS, TILES * TB), BF16),
            pltpu.VMEM((Y, COLS, TILES * TB), BF16),
            pltpu.SemaphoreType.DMA((10,)),
            *pair(len(Z_PLAN)),
            *pair(PLANE),
            *pair(Y),
            *pair(4),
            *pair(2, PLANE),
            *pair(2, PLANE),
            *pair(len(N_PLAN)),
            *pair(4),
            *pair(2),
            *pair(Y),
            *pair(PLANE),
            *pair(Z),
        ],
        compiler_params=pltpu.CompilerParams(
            collective_id=0, has_side_effects=True, vmem_limit_bytes=60 * 2**20),
        name="exchange",
    )(
        x_cols, q_cols, halo_ids, obs_prec, tile_owner.reshape(1, TILES), tile_sub.reshape(1, TILES),
        q_tiles, a_tiles,
    )
    return product, gram.T


def solution(mesh):
    torus = Mesh(mesh.devices.reshape(Z, X, C, Y), ("z", "x", "core", "col"))
    parts = ("z", "x", "core")
    in_specs = (
        P("col", parts),
        P(parts, None, None),
        P(parts, None),
        P(parts, None),
        P(parts, None, None),
        P(parts, None),
        P(parts, None),
        P(parts),
    )
    out_specs = (P("col", parts), P(None, "col"))
    return jax.shard_map(body, mesh=torus, in_specs=in_specs, out_specs=out_specs, check_vma=False)
```

```python
import math

import jax
import jax.numpy as jnp
from jax import lax
from jax.experimental import pallas as pl
from jax.experimental.pallas import tpu as pltpu
from jax.sharding import Mesh
from jax.sharding import PartitionSpec as P

LOGICAL = pl.DeviceIdType.MESH
Z, X, C, Y = 16, 4, 2, 4
PLANE = X * C
PARTS = Z * PLANE
TB = 128
COLS = 8
RB = 8
NB = 5
TILES = 64
SLOTS = 2 * Z
F32 = jnp.float32
BF16 = jnp.bfloat16
GROUP = 8
Z_PLAN = [(0, 5, None), (0, -5, None), (0, 1, None), (0, -1, None), (0, 2, None), (0, -2, None)]
Z_OWN = len(Z_PLAN)
Z_PLAN += [(-5, 3, 0), (-5, 2, None), (-5, -2, None), (-5, 1, None), (-5, -1, None)]
Z_PLAN += [(5, -3, 1), (5, 2, None), (5, -2, None), (5, 1, None), (5, -1, None)]
ORDER = (0, 1, 15, 2, 14, 5, 11, 3, 4, 6, 7, 8, 9, 10, 12, 13)
FIRST = 7
WAVES = ((0, FIRST), (FIRST, Z))
N_PLAN = [(8, -3, 0), (13, 2, None), (9, -2, None), (12, 1, None), (10, -1, None)]
N_PLAN += [(8, 3, 1), (7, 2, None), (3, -2, None), (6, 1, None), (4, -1, None)]
NT = (((1,), (1,)), ((), ()))
NN = (((1,), (0,)), ((), ()))


def kernel(
    x_hbm, qc_hbm, halo_hbm, prec_hbm, owner_hbm, sub_hbm, q_hbm, a_hbm,
    y_ref, g_ref,
    x_v, qc_s, halo_s, prec_in, own_v, sub_v,
    q_v, a_v, win, mine, share, zx, zy, xy, req, meta, req_s, meta_s, stage, xs, cb, stage2, rc, dn, near, csum, direct,
    far, acc, g1, g2, gp, prec, pb, wb, pg,
    loc_sem, s_z, r_z, s_q, r_q, s_y, r_y, s_h, r_h, s_p, r_p, s_c, r_c, s_n, r_n, s_d, r_d, s_f, r_f, s_j, r_j,
    s_g1, r_g1, s_g2, r_g2,
):
    z, x, c, y = (lax.axis_index(n) for n in ("z", "x", "core", "col"))
    mq = x * C + c
    me = z * PLANE + mq

    def round_z(d):
        return lax.rem(z + d + Z, Z)

    def at_z(d):
        return {"z": round_z(d)}

    def plane_peer(k):
        px, pc = lax.rem(x + k // C, X), lax.rem(c + k % C, C)
        return {"x": px, "core": pc}, px * C + pc

    def at_part(d):
        p = lax.rem(me + d + PARTS, PARTS)
        return {"z": p // PLANE, "x": lax.rem(p // C, X), "core": lax.rem(p, C)}

    def at_y(d):
        return {"col": lax.rem(y + d, Y)}

    def send(src, dst, sems, i, where):
        return pltpu.make_async_remote_copy(
            src_ref=src, dst_ref=dst, send_sem=sems[0].at[i], recv_sem=sems[1].at[i],
            device_id=where, device_id_type=LOGICAL,
        )

    def start(copies):
        for copy in copies:
            copy.start()
        return copies

    def finish(copies):
        for copy in copies:
            copy.wait()

    loads = [
        pltpu.make_async_copy(src, dst, loc_sem.at[i])
        for i, (src, dst) in enumerate((
            (x_hbm, x_v), (halo_hbm, halo_s), (owner_hbm, own_v), (sub_hbm, sub_v), (prec_hbm, prec_in),
            (qc_hbm, qc_s), (q_hbm, q_v), (a_hbm, a_v),
        ))
    ]
    start(loads)
    x_in, halo_in, own_in, sub_in, prec_load, qc_in, q_in, a_in = loads

    barrier = pltpu.get_barrier_semaphore()
    halo_steps = (2, 1, -1, -2)
    others = [at_z(d) for d in range(1, Z)] + [plane_peer(k)[0] for k in range(1, PLANE)]
    others += [at_part(d) for d in halo_steps] + [at_y(d) for d in range(1, Y)]
    for other in others:
        pl.semaphore_signal(barrier, inc=1, device_id=other, device_id_type=LOGICAL)

    x_in.wait()
    halo_in.wait()
    for r in range(RB):
        block = x_v[:, r * TB:(r + 1) * TB]
        win[r] = block
        mine[r] = block
        zx[0, r] = block
    xy[y] = x_v[...]
    for h in range(2):
        share[h] = mine[halo_s[0, h]]

    def chunk(d):
        i = ORDER.index(d % Z)
        return zx.at[i] if i < FIRST else zy.at[i - FIRST]

    def z_copy(i):
        hold, step, half = Z_PLAN[i]
        src, dst = chunk(hold), chunk(hold - step)
        if half is not None:
            rows = pl.ds(half * (RB // 2), RB // 2)
            src, dst = src.at[rows], dst.at[rows]
        return send(src, dst, (s_z, r_z), i, at_z(step))

    z_copies = [z_copy(i) for i in range(len(Z_PLAN))]

    pl.semaphore_wait(barrier, len(others))

    start(z_copies[:Z_OWN])
    halos = start([
        send(share, win.at[pl.ds(RB + 2 * m, 2)], (s_h, r_h), m, at_part(d))
        for m, d in enumerate(halo_steps)
    ])
    probes = start([send(x_v, xy.at[y], (s_y, r_y), d, at_y(d)) for d in range(1, Y)])

    own_in.wait()
    sub_in.wait()
    prec_load.wait()
    prec[...] = prec_in[...].astype(F32)
    shape = (TILES, TB)
    lane = lax.broadcasted_iota(jnp.int32, shape, 1)
    row = lax.broadcasted_iota(jnp.int32, shape, 0)
    eye = lane == row
    fill = jnp.full((1, TB - TILES), -1, jnp.int32)
    own_r = jnp.concatenate([own_v[...], fill], axis=1)
    sub_r = jnp.concatenate([sub_v[...], fill], axis=1)
    own_b = jnp.broadcast_to(jnp.sum(jnp.where(eye, own_r, 0), axis=1, keepdims=True), shape)
    sub_b = jnp.broadcast_to(jnp.sum(jnp.where(eye, sub_r, 0), axis=1, keepdims=True), shape)
    same = own_b == own_r
    j_b = jnp.broadcast_to(
        jnp.sum(jnp.where(same & (lane < row), 1, 0), axis=1, keepdims=True), shape)
    j_r = jnp.sum(jnp.where(same & (row < lane), 1, 0), axis=0, keepdims=True)
    col_b = jnp.bitwise_and(own_b, PLANE - 1)

    def place_of(owner):
        offset = jnp.bitwise_and(jnp.right_shift(owner, 3) - z, Z - 1)
        return sum(jnp.where(offset == d, 2 * i, 0) for i, d in enumerate(ORDER) if i)

    key_b = place_of(own_b) + j_b
    for q in range(PLANE):
        hit = (col_b == q) & (key_b == lane)
        wanted = jnp.sum(jnp.where(hit, sub_b + 1, 0), axis=0, keepdims=True) - 1
        req[mq, q:q + 1] = wanted
        meta[PLANE + q:PLANE + q + 1] = jnp.sum(jnp.where(hit, row - TILES, 0), axis=0, keepdims=True) + TILES
    slot_r = jnp.bitwise_and(own_r, PLANE - 1) * SLOTS + place_of(own_r) + j_r
    meta[:PLANE] = jnp.broadcast_to(slot_r, (8, TB))
    to_meta = pltpu.make_async_copy(meta, meta_s, loc_sem.at[8])
    to_meta.start()
    asks = start([send(req.at[mq], req.at[mq], (s_q, r_q), k, plane_peer(k)[0]) for k in range(1, PLANE)])

    for i in range(2):
        z_copies[i].wait_recv()
        start(z_copies[Z_OWN + 5 * i:Z_OWN + 5 * i + 5])

    finish(asks)
    to_req = pltpu.make_async_copy(req, req_s, loc_sem.at[9])
    to_req.start()
    for copy in z_copies[2:Z_OWN]:
        copy.wait_recv()
    to_req.wait()

    def give(wave, k):
        low, high = WAVES[wave]
        slots = pl.ds(2 * low, 2 * (high - low))
        return send(stage.at[k, slots], xs.at[mq, slots], (s_p.at[wave], r_p.at[wave]), k, plane_peer(k)[0])

    def pick(wave, k, dst):
        _, q = plane_peer(k)
        held, low = (zy, FIRST) if wave else (zx, 0)
        for i in range(*WAVES[wave]):
            for j in range(2):
                dst[2 * i + j] = held[i - low, jnp.maximum(req_s[q, mq, 2 * i + j], 0)]

    for wave in range(2):
        if wave:
            for copy in z_copies[Z_OWN:]:
                copy.wait_recv()

        def hand_out(i, carry, wave=wave):
            k = lax.rem(i + 3, PLANE - 1) + 1
            pick(wave, k, stage.at[k])
            give(wave, k).start()
            return carry

        lax.fori_loop(0, PLANE - 1, hand_out, 0)
        pick(wave, 0, xs.at[mq])
    to_meta.wait()
    a_in.wait()
    for copy in z_copies:
        copy.wait_send()
    for wave in range(2):
        finish([give(wave, k) for k in range(1, PLANE)])

    xs_flat = xs.reshape(PLANE * SLOTS, COLS, TB)

    def terms(group, carry):
        base = pl.multiple_of(group * GROUP, GROUP)
        scales = prec[pl.ds(base, GROUP), :]
        tiles, projected, weighted = [], [], []
        for i in range(0, GROUP, 2):
            tile = a_v[pl.ds(base + i, 2)].reshape(2 * TB, TB)
            pair = jnp.concatenate([xs_flat[meta_s[0, base + i]], xs_flat[meta_s[0, base + i + 1]]], axis=0)
            tiles.append(tile)
            projected.append(lax.dot_general(pair, tile, NT, preferred_element_type=F32))
        zero = jnp.zeros((COLS, TB), F32)
        for i in range(0, GROUP, 2):
            both = projected[i // 2]
            top, low = both[:COLS, :TB], both[COLS:, TB:]
            top_w, low_w = scales[i:i + 1] * top, scales[i + 1:i + 2] * low
            block = jnp.concatenate([
                jnp.concatenate([top_w, zero], axis=1), jnp.concatenate([zero, low_w], axis=1)], axis=0)
            weighted.append(block.astype(BF16))
            for h, (p, w) in enumerate(((top, top_w), (low, low_w))):
                lanes = pl.ds(pl.multiple_of((base + i + h) * TB, TB), TB)
                pb[:, lanes] = p.astype(BF16)
                wb[:, lanes] = w.astype(BF16)
        for i in range(0, GROUP, 2):
            both = lax.dot_general(weighted[i // 2], tiles[i // 2], NN, preferred_element_type=F32)
            cb[base + i] = both[:COLS]
            cb[base + i + 1] = both[COLS:]
        return carry

    lax.fori_loop(0, TILES // GROUP, terms, 0)
    cb[TILES] = jnp.zeros((COLS, TB), F32)
    turns = start([send(pb, pg.at[y], (s_j, r_j), d, at_y(d)) for d in range(1, Y)])

    def back(wave, k):
        low, high = WAVES[wave]
        slots = pl.ds(2 * low, 2 * (high - low))
        return send(stage2.at[k, slots], rc.at[mq, slots], (s_c.at[wave], r_c.at[wave]), k, plane_peer(k)[0])

    def place(wave, k, dst):
        _, q = plane_peer(k)
        for i in range(2 * WAVES[wave][0], 2 * WAVES[wave][1]):
            dst[i] = cb[meta_s[PLANE + q, i]]

    for wave in (1, 0):

        def hand_back(i, carry, wave=wave):
            k = lax.rem(i + 3, PLANE - 1) + 1
            place(wave, k, stage2.at[k])
            back(wave, k).start()
            return carry

        lax.fori_loop(0, PLANE - 1, hand_back, 0)
        place(wave, 0, rc.at[mq])

    pg[y] = pb[...]
    finish(halos)
    qc_in.wait()
    q_in.wait()

    def prior(r, carry):
        total = jnp.zeros((COLS, TB), F32)
        for k in range(NB):
            total += lax.dot_general(win[qc_s[r, k]], q_v[r * NB + k], NT, preferred_element_type=F32)
        acc[r] = total
        return carry

    lax.fori_loop(0, RB, prior, 0, unroll=4)
    finish(probes)
    part = jnp.zeros((COLS, COLS * Y), F32)
    for r in range(RB):
        across = jnp.concatenate([xy[i, :, r * TB:(r + 1) * TB] for i in range(Y)], axis=0)
        part += lax.dot_general(
            acc[r], across.astype(F32), NT, precision=lax.Precision.HIGHEST, preferred_element_type=F32)
    finish(turns)

    def gram_part(i, part):
        lanes = pl.ds(pl.multiple_of(i * 1024, 1024), 1024)
        across = jnp.concatenate([pg[j, :, lanes] for j in range(Y)], axis=0)
        return part + lax.dot_general(wb[:, lanes], across, NT, preferred_element_type=F32)

    part = lax.fori_loop(0, TILES * TB // 1024, gram_part, part)
    gp[...] = jnp.concatenate([part[2 * i:2 * i + 2] for i in range(COLS // 2)], axis=1)
    firsts = start([send(gp, g1.at[k], (s_g1, r_g1), k, plane_peer(k)[0]) for k in range(1, PLANE)])
    g1[0] = gp[...]

    def dense(i, carry):
        totals = [jnp.zeros((COLS, TB), F32) for _ in range(RB)]
        for q in range(PLANE):
            for j in range(2):
                sub = jnp.broadcast_to(req_s[q, mq, 2 * i + j], (COLS, TB))
                block = rc[q, 2 * i + j]
                totals = [total + jnp.where(sub == r, block, 0.0) for r, total in enumerate(totals)]
        for r in range(RB):
            dn[i, r] = totals[r]
        return carry

    def sums_for(d):
        return dn.at[ORDER.index(d % Z)]

    finish([back(1, k) for k in range(1, PLANE)])
    lax.fori_loop(*WAVES[1], dense, 0)
    nears = []
    for i, (d, step, half) in enumerate(N_PLAN):
        src, dst = sums_for(d), near.at[i]
        if half is not None:
            rows = pl.ds(half * (RB // 2), RB // 2)
            src, dst = src.at[rows], dst.at[rows]
        nears += start([send(src, dst, (s_n, r_n), i, at_z(step))])
    finish(firsts)
    g2[0] = jnp.sum(g1[...], axis=0)
    seconds = start([send(g2.at[0], g2.at[d], (s_g2, r_g2), d, at_z(d)) for d in range(1, Z)])
    finish([back(0, k) for k in range(1, PLANE)])
    lax.fori_loop(*WAVES[0], dense, 0)
    directs = start([send(sums_for(d), direct.at[i], (s_d, r_d), i, at_z(d)) for i, d in enumerate((1, -1, 2, -2))])
    finish(nears)
    fars = []
    for g, d in enumerate((-5, 5)):
        for r in range(RB):
            total = sums_for(d)[r]
            for i in range(4):
                total += near[5 * g + 1 + i, r]
            if r // (RB // 2) == g:
                total += near[5 * g, r]
            csum[g, r] = total
        fars += start([send(csum.at[g], far.at[g], (s_f, r_f), g, at_z(d))])
    finish(directs)
    for r in range(RB):
        acc[r] += (dn[0, r] + direct[0, r]) + (direct[1, r] + direct[2, r]) + direct[3, r]
    finish(seconds)
    total = jnp.sum(g2[...], axis=0) * (1.0 / math.sqrt(RB * TB * PARTS))
    width = COLS * Y
    g_ref[...] = jnp.concatenate([total[:, i * width:(i + 1) * width] for i in range(COLS // 2)], axis=0)
    finish(fars)
    for r in range(RB):
        y_ref[:, r * TB:(r + 1) * TB] = acc[r] + (far[0, r] + far[1, r])


def settle(product_ref, gram_ref, y_ref, g_ref):
    y_ref[...] = product_ref[...]
    g_ref[...] = gram_ref[...]


def body(x_cols, q_tiles, q_cols, halo_ids, a_tiles, obs_prec, tile_owner, tile_sub):
    vmem = pl.BlockSpec(memory_space=pltpu.VMEM)
    hbm = pl.BlockSpec(memory_space=pl.ANY)
    block = (COLS, TB)

    def pair(*shape):
        return [pltpu.SemaphoreType.DMA(shape)] * 2

    product, gram = pl.pallas_call(
        kernel,
        out_shape=(
            jax.ShapeDtypeStruct((COLS, RB * TB), F32),
            jax.ShapeDtypeStruct((COLS, COLS * Y), F32),
        ),
        in_specs=[hbm] * 8,
        out_specs=(vmem, vmem),
        scratch_shapes=[
            pltpu.VMEM((COLS, RB * TB), BF16),
            pltpu.SMEM((RB, NB), jnp.int32),
            pltpu.SMEM((1, 2), jnp.int32),
            pltpu.VMEM((TILES, TB), BF16),
            pltpu.VMEM((1, TILES), jnp.int32),
            pltpu.VMEM((1, TILES), jnp.int32),
            pltpu.VMEM((RB * NB, TB, TB), BF16),
            pltpu.VMEM((TILES, TB, TB), BF16),
            pltpu.VMEM((RB + 8, *block), BF16),
            pltpu.VMEM((RB, *block), BF16),
            pltpu.VMEM((2, *block), BF16),
            pltpu.VMEM((FIRST, RB, *block), BF16),
            pltpu.VMEM((Z - FIRST, RB, *block), BF16),
            pltpu.VMEM((Y, COLS, RB * TB), BF16),
            pltpu.VMEM((PLANE, PLANE, TB), jnp.int32),
            pltpu.VMEM((2 * PLANE, TB), jnp.int32),
            pltpu.SMEM((PLANE, PLANE, TB), jnp.int32),
            pltpu.SMEM((2 * PLANE, TB), jnp.int32),
            pltpu.VMEM((PLANE, SLOTS, *block), BF16),
            pltpu.VMEM((PLANE, SLOTS, *block), BF16),
            pltpu.VMEM((TILES + 1, *block), F32),
            pltpu.VMEM((PLANE, SLOTS, *block), F32),
            pltpu.VMEM((PLANE, SLOTS, *block), F32),
            pltpu.VMEM((Z, RB, *block), F32),
            pltpu.VMEM((len(N_PLAN), RB, *block), F32),
            pltpu.VMEM((2, RB, *block), F32),
            pltpu.VMEM((4, RB, *block), F32),
            pltpu.VMEM((2, RB, *block), F32),
            pltpu.VMEM((RB, *block), F32),
            pltpu.VMEM((PLANE, 2, TB), F32),
            pltpu.VMEM((Z, 2, TB), F32),
            pltpu.VMEM((2, TB), F32),
            pltpu.VMEM((TILES, TB), F32),
            pltpu.VMEM((COLS, TILES * TB), BF16),
            pltpu.VMEM((COLS, TILES * TB), BF16),
            pltpu.VMEM((Y, COLS, TILES * TB), BF16),
            pltpu.SemaphoreType.DMA((10,)),
            *pair(len(Z_PLAN)),
            *pair(PLANE),
            *pair(Y),
            *pair(4),
            *pair(2, PLANE),
            *pair(2, PLANE),
            *pair(len(N_PLAN)),
            *pair(4),
            *pair(2),
            *pair(Y),
            *pair(PLANE),
            *pair(Z),
        ],
        compiler_params=pltpu.CompilerParams(
            collective_id=0, has_side_effects=True, vmem_limit_bytes=60 * 2**20),
        name="exchange",
    )(
        x_cols, q_cols, halo_ids, obs_prec, tile_owner.reshape(1, TILES), tile_sub.reshape(1, TILES),
        q_tiles, a_tiles,
    )
    product, gram = pl.pallas_call(
        settle,
        out_shape=(jax.ShapeDtypeStruct(product.shape, F32), jax.ShapeDtypeStruct(gram.shape, F32)),
        name="settle",
    )(product, gram)
    return product, gram.T


def solution(mesh):
    torus = Mesh(mesh.devices.reshape(Z, X, C, Y), ("z", "x", "core", "col"))
    parts = ("z", "x", "core")
    in_specs = (
        P("col", parts),
        P(parts, None, None),
        P(parts, None),
        P(parts, None),
        P(parts, None, None),
        P(parts, None),
        P(parts, None),
        P(parts),
    )
    out_specs = (P("col", parts), P(None, "col"))
    return jax.shard_map(body, mesh=torus, in_specs=in_specs, out_specs=out_specs, check_vma=False)
```

```python
import math

import jax
import jax.numpy as jnp
from jax import lax
from jax.experimental import pallas as pl
from jax.experimental.pallas import tpu as pltpu
from jax.sharding import Mesh
from jax.sharding import PartitionSpec as P

LOGICAL = pl.DeviceIdType.MESH
Z, X, C, Y = 16, 4, 2, 4
PLANE = X * C
PARTS = Z * PLANE
TB = 128
COLS = 8
RB = 8
NB = 5
TILES = 64
SLOTS = 2 * Z
F32 = jnp.float32
BF16 = jnp.bfloat16
GROUP = 32
LEVELS = 32767.0
Z_PLAN = [(0, 5, None), (0, -5, None), (0, 1, None), (0, -1, None), (0, 2, None), (0, -2, None)]
Z_OWN = len(Z_PLAN)
Z_PLAN += [(-5, 3, 0), (-5, 2, None), (-5, -2, None), (-5, 1, None), (-5, -1, None)]
Z_PLAN += [(5, -3, 1), (5, 2, None), (5, -2, None), (5, 1, None), (5, -1, None)]
ORDER = (0, 1, 15, 2, 14, 5, 11, 3, 4, 6, 7, 8, 9, 10, 12, 13)
FIRST = 7
WAVES = ((0, FIRST), (FIRST, Z))
N_PLAN = [(8, -3, 0), (13, 2, None), (9, -2, None), (12, 1, None), (10, -1, None)]
N_PLAN += [(8, 3, 1), (7, 2, None), (3, -2, None), (6, 1, None), (4, -1, None)]
NT = (((1,), (1,)), ((), ()))
NN = (((1,), (0,)), ((), ()))


def kernel(
    x_hbm, qc_hbm, halo_hbm, prec_hbm, owner_hbm, sub_hbm, q_hbm, a_hbm,
    y_ref, g_ref,
    x_v, qc_s, halo_s, prec_in, own_v, sub_v,
    q_v, a_v, win, mine, share, zx, zy, xy, req, meta, req_s, meta_s, stage, xs, cb, stage2, rc,
    coded, unit_out, unit_in, dn, near, csum, direct,
    far, acc, g1, g2, gp, prec, pb, wb, pg,
    loc_sem, s_z, r_z, s_q, r_q, s_y, r_y, s_h, r_h, s_p, r_p, s_c, r_c, s_u, r_u, s_n, r_n, s_d, r_d, s_f, r_f, s_j, r_j,
    s_g1, r_g1, s_g2, r_g2,
):
    z, x, c, y = (lax.axis_index(n) for n in ("z", "x", "core", "col"))
    mq = x * C + c
    me = z * PLANE + mq

    def round_z(d):
        return lax.rem(z + d + Z, Z)

    def at_z(d):
        return {"z": round_z(d)}

    def plane_peer(k):
        px, pc = lax.rem(x + k // C, X), lax.rem(c + k % C, C)
        return {"x": px, "core": pc}, px * C + pc

    def at_part(d):
        p = lax.rem(me + d + PARTS, PARTS)
        return {"z": p // PLANE, "x": lax.rem(p // C, X), "core": lax.rem(p, C)}

    def at_y(d):
        return {"col": lax.rem(y + d, Y)}

    def send(src, dst, sems, i, where):
        return pltpu.make_async_remote_copy(
            src_ref=src, dst_ref=dst, send_sem=sems[0].at[i], recv_sem=sems[1].at[i],
            device_id=where, device_id_type=LOGICAL,
        )

    def start(copies):
        for copy in copies:
            copy.start()
        return copies

    def finish(copies):
        for copy in copies:
            copy.wait()

    loads = [
        pltpu.make_async_copy(src, dst, loc_sem.at[i])
        for i, (src, dst) in enumerate((
            (x_hbm, x_v), (halo_hbm, halo_s), (owner_hbm, own_v), (sub_hbm, sub_v), (prec_hbm, prec_in),
            (qc_hbm, qc_s), (q_hbm, q_v), (a_hbm, a_v),
        ))
    ]
    start(loads)
    x_in, halo_in, own_in, sub_in, prec_load, qc_in, q_in, a_in = loads

    barrier = pltpu.get_barrier_semaphore()
    halo_steps = (2, 1, -1, -2)
    others = [at_z(d) for d in range(1, Z)] + [plane_peer(k)[0] for k in range(1, PLANE)]
    others += [at_part(d) for d in halo_steps] + [at_y(d) for d in range(1, Y)]
    for other in others:
        pl.semaphore_signal(barrier, inc=1, device_id=other, device_id_type=LOGICAL)

    x_in.wait()
    halo_in.wait()
    for r in range(RB):
        block = x_v[:, r * TB:(r + 1) * TB]
        win[r] = block
        mine[r] = block
        zx[0, r] = block
    xy[y] = x_v[...]
    for h in range(2):
        share[h] = mine[halo_s[0, h]]

    def chunk(d):
        i = ORDER.index(d % Z)
        return zx.at[i] if i < FIRST else zy.at[i - FIRST]

    def z_copy(i):
        hold, step, half = Z_PLAN[i]
        src, dst = chunk(hold), chunk(hold - step)
        if half is not None:
            rows = pl.ds(half * (RB // 2), RB // 2)
            src, dst = src.at[rows], dst.at[rows]
        return send(src, dst, (s_z, r_z), i, at_z(step))

    z_copies = [z_copy(i) for i in range(len(Z_PLAN))]

    pl.semaphore_wait(barrier, len(others))

    start(z_copies[:Z_OWN])
    halos = start([
        send(share, win.at[pl.ds(RB + 2 * m, 2)], (s_h, r_h), m, at_part(d))
        for m, d in enumerate(halo_steps)
    ])
    probes = start([send(x_v, xy.at[y], (s_y, r_y), d, at_y(d)) for d in range(1, Y)])

    own_in.wait()
    sub_in.wait()
    prec_load.wait()
    prec[...] = prec_in[...].astype(F32)
    shape = (TILES, TB)
    lane = lax.broadcasted_iota(jnp.int32, shape, 1)
    row = lax.broadcasted_iota(jnp.int32, shape, 0)
    eye = lane == row
    fill = jnp.full((1, TB - TILES), -1, jnp.int32)
    own_r = jnp.concatenate([own_v[...], fill], axis=1)
    sub_r = jnp.concatenate([sub_v[...], fill], axis=1)
    own_b = jnp.broadcast_to(jnp.sum(jnp.where(eye, own_r, 0), axis=1, keepdims=True), shape)
    sub_b = jnp.broadcast_to(jnp.sum(jnp.where(eye, sub_r, 0), axis=1, keepdims=True), shape)
    same = own_b == own_r
    j_b = jnp.broadcast_to(
        jnp.sum(jnp.where(same & (lane < row), 1, 0), axis=1, keepdims=True), shape)
    j_r = jnp.sum(jnp.where(same & (row < lane), 1, 0), axis=0, keepdims=True)
    col_b = jnp.bitwise_and(own_b, PLANE - 1)

    def place_of(owner):
        offset = jnp.bitwise_and(jnp.right_shift(owner, 3) - z, Z - 1)
        return sum(jnp.where(offset == d, 2 * i, 0) for i, d in enumerate(ORDER) if i)

    key_b = place_of(own_b) + j_b
    for q in range(PLANE):
        hit = (col_b == q) & (key_b == lane)
        wanted = jnp.sum(jnp.where(hit, sub_b + 1, 0), axis=0, keepdims=True) - 1
        req[mq, q:q + 1] = wanted
        meta[PLANE + q:PLANE + q + 1] = jnp.sum(jnp.where(hit, row - TILES, 0), axis=0, keepdims=True) + TILES
    slot_r = jnp.bitwise_and(own_r, PLANE - 1) * SLOTS + place_of(own_r) + j_r
    meta[:PLANE] = jnp.broadcast_to(slot_r, (8, TB))
    to_meta = pltpu.make_async_copy(meta, meta_s, loc_sem.at[8])
    to_meta.start()
    asks = start([send(req.at[mq], req.at[mq], (s_q, r_q), k, plane_peer(k)[0]) for k in range(1, PLANE)])

    for i in range(2):
        z_copies[i].wait_recv()
        start(z_copies[Z_OWN + 5 * i:Z_OWN + 5 * i + 5])

    finish(asks)
    to_req = pltpu.make_async_copy(req, req_s, loc_sem.at[9])
    to_req.start()
    for copy in z_copies[2:Z_OWN]:
        copy.wait_recv()
    to_req.wait()

    def give(wave, k):
        low, high = WAVES[wave]
        slots = pl.ds(2 * low, 2 * (high - low))
        return send(stage.at[k, slots], xs.at[mq, slots], (s_p.at[wave], r_p.at[wave]), k, plane_peer(k)[0])

    def pick(wave, k, dst):
        _, q = plane_peer(k)
        held, low = (zy, FIRST) if wave else (zx, 0)
        for i in range(*WAVES[wave]):
            for j in range(2):
                dst[2 * i + j] = held[i - low, jnp.maximum(req_s[q, mq, 2 * i + j], 0)]

    for wave in range(2):
        if wave:
            for copy in z_copies[Z_OWN:]:
                copy.wait_recv()

        def hand_out(i, carry, wave=wave):
            k = lax.rem(i + 3, PLANE - 1) + 1
            pick(wave, k, stage.at[k])
            give(wave, k).start()
            return carry

        lax.fori_loop(0, PLANE - 1, hand_out, 0)
        pick(wave, 0, xs.at[mq])
    to_meta.wait()
    a_in.wait()
    for copy in z_copies:
        copy.wait_send()
    for wave in range(2):
        finish([give(wave, k) for k in range(1, PLANE)])

    xs_flat = xs.reshape(PLANE * SLOTS, COLS, TB)

    def terms(group, carry):
        base = pl.multiple_of(group * GROUP, GROUP)
        scales = prec[pl.ds(base, GROUP), :]
        tiles, projected, weighted = [], [], []
        for i in range(0, GROUP, 2):
            tile = a_v[pl.ds(base + i, 2)].reshape(2 * TB, TB)
            pair = jnp.concatenate([xs_flat[meta_s[0, base + i]], xs_flat[meta_s[0, base + i + 1]]], axis=0)
            tiles.append(tile)
            projected.append(lax.dot_general(pair, tile, NT, preferred_element_type=F32))
        zero = jnp.zeros((COLS, TB), F32)
        for i in range(0, GROUP, 2):
            both = projected[i // 2]
            top, low = both[:COLS, :TB], both[COLS:, TB:]
            top_w, low_w = scales[i:i + 1] * top, scales[i + 1:i + 2] * low
            block = jnp.concatenate([
                jnp.concatenate([top_w, zero], axis=1), jnp.concatenate([zero, low_w], axis=1)], axis=0)
            weighted.append(block.astype(BF16))
            for h, (p, w) in enumerate(((top, top_w), (low, low_w))):
                lanes = pl.ds(pl.multiple_of((base + i + h) * TB, TB), TB)
                pb[:, lanes] = p.astype(BF16)
                wb[:, lanes] = w.astype(BF16)
        for i in range(0, GROUP, 2):
            both = lax.dot_general(weighted[i // 2], tiles[i // 2], NN, preferred_element_type=F32)
            cb[base + i] = both[:COLS]
            cb[base + i + 1] = both[COLS:]
            carry = jnp.maximum(carry, jnp.maximum(jnp.abs(both[:COLS]), jnp.abs(both[COLS:])))
        return carry

    largest = lax.fori_loop(0, TILES // GROUP, terms, jnp.zeros((COLS, TB), F32))
    turns = start([send(pb, pg.at[y], (s_j, r_j), d, at_y(d)) for d in range(1, Y)])

    largest = jnp.broadcast_to(jnp.max(largest, axis=1, keepdims=True), (COLS, TB))
    unit_out[...] = largest * (1.0 / LEVELS)
    unit_in[mq] = unit_out[...]
    units = start([send(unit_out, unit_in.at[mq], (s_u, r_u), k, plane_peer(k)[0]) for k in range(1, PLANE)])
    per_unit = LEVELS / jnp.maximum(largest, 1e-30)

    def code(group, carry):
        for i in range(GROUP):
            t = group * GROUP + i
            coded[t] = jnp.floor(cb[t] * per_unit + 0.5).astype(jnp.int32).astype(jnp.int16)
        return carry

    lax.fori_loop(0, TILES // GROUP, code, 0)
    coded[TILES] = jnp.zeros((COLS, TB), jnp.int16)

    def back(wave, k):
        low, high = WAVES[wave]
        slots = pl.ds(2 * low, 2 * (high - low))
        return send(stage2.at[k, slots], rc.at[mq, slots], (s_c.at[wave], r_c.at[wave]), k, plane_peer(k)[0])

    def place(wave, k, dst):
        _, q = plane_peer(k)
        for i in range(2 * WAVES[wave][0], 2 * WAVES[wave][1]):
            dst[i] = coded[meta_s[PLANE + q, i]]

    for wave in (1, 0):

        def hand_back(i, carry, wave=wave):
            k = lax.rem(i + 3, PLANE - 1) + 1
            place(wave, k, stage2.at[k])
            back(wave, k).start()
            return carry

        lax.fori_loop(0, PLANE - 1, hand_back, 0)
        place(wave, 0, rc.at[mq])

    pg[y] = pb[...]
    finish(halos)
    qc_in.wait()
    q_in.wait()

    def prior(r, carry):
        total = jnp.zeros((COLS, TB), F32)
        for k in range(NB):
            total += lax.dot_general(win[qc_s[r, k]], q_v[r * NB + k], NT, preferred_element_type=F32)
        acc[r] = total
        return carry

    lax.fori_loop(0, RB, prior, 0, unroll=4)
    def dense(i, carry):
        totals = [jnp.zeros((COLS, TB), F32) for _ in range(RB)]
        for q in range(PLANE):
            unit = unit_in[q]
            for j in range(2):
                sub = jnp.broadcast_to(req_s[q, mq, 2 * i + j], (COLS, TB))
                block = rc[q, 2 * i + j].astype(jnp.int32).astype(F32) * unit
                totals = [total + jnp.where(sub == r, block, 0.0) for r, total in enumerate(totals)]
        for r in range(RB):
            dn[i, r] = totals[r]
        return carry

    def sums_for(d):
        return dn.at[ORDER.index(d % Z)]

    finish(units)
    finish([back(1, k) for k in range(1, PLANE)])
    lax.fori_loop(*WAVES[1], dense, 0)
    nears = []
    for i, (d, step, half) in enumerate(N_PLAN):
        src, dst = sums_for(d), near.at[i]
        if half is not None:
            rows = pl.ds(half * (RB // 2), RB // 2)
            src, dst = src.at[rows], dst.at[rows]
        nears += start([send(src, dst, (s_n, r_n), i, at_z(step))])
    finish(probes)
    part = jnp.zeros((COLS, COLS * Y), F32)
    for r in range(RB):
        across = jnp.concatenate([xy[i, :, r * TB:(r + 1) * TB] for i in range(Y)], axis=0)
        part += lax.dot_general(
            acc[r], across.astype(F32), NT, precision=lax.Precision.HIGHEST, preferred_element_type=F32)
    finish(turns)

    def gram_part(i, part):
        lanes = pl.ds(pl.multiple_of(i * 1024, 1024), 1024)
        across = jnp.concatenate([pg[j, :, lanes] for j in range(Y)], axis=0)
        return part + lax.dot_general(wb[:, lanes], across, NT, preferred_element_type=F32)

    part = lax.fori_loop(0, TILES * TB // 1024, gram_part, part)
    gp[...] = jnp.concatenate([part[2 * i:2 * i + 2] for i in range(COLS // 2)], axis=1)
    firsts = start([send(gp, g1.at[k], (s_g1, r_g1), k, plane_peer(k)[0]) for k in range(1, PLANE)])
    g1[0] = gp[...]

    finish([back(0, k) for k in range(1, PLANE)])
    lax.fori_loop(*WAVES[0], dense, 0)
    directs = start([send(sums_for(d), direct.at[i], (s_d, r_d), i, at_z(d)) for i, d in enumerate((1, -1, 2, -2))])
    finish(firsts)
    g2[0] = jnp.sum(g1[...], axis=0)
    seconds = start([send(g2.at[0], g2.at[d], (s_g2, r_g2), d, at_z(d)) for d in range(1, Z)])
    finish(nears)
    fars = []
    for g, d in enumerate((-5, 5)):
        for r in range(RB):
            total = sums_for(d)[r]
            for i in range(4):
                total += near[5 * g + 1 + i, r]
            if r // (RB // 2) == g:
                total += near[5 * g, r]
            csum[g, r] = total
        fars += start([send(csum.at[g], far.at[g], (s_f, r_f), g, at_z(d))])
    finish(directs)
    for r in range(RB):
        acc[r] += (dn[0, r] + direct[0, r]) + (direct[1, r] + direct[2, r]) + direct[3, r]
    finish(seconds)
    total = jnp.sum(g2[...], axis=0) * (1.0 / math.sqrt(RB * TB * PARTS))
    width = COLS * Y
    g_ref[...] = jnp.concatenate([total[:, i * width:(i + 1) * width] for i in range(COLS // 2)], axis=0)
    finish(fars)
    for r in range(RB):
        y_ref[:, r * TB:(r + 1) * TB] = acc[r] + (far[0, r] + far[1, r])


def settle(product_ref, gram_ref, y_ref, g_ref):
    y_ref[...] = product_ref[...]
    g_ref[...] = gram_ref[...]


def body(x_cols, q_tiles, q_cols, halo_ids, a_tiles, obs_prec, tile_owner, tile_sub):
    vmem = pl.BlockSpec(memory_space=pltpu.VMEM)
    hbm = pl.BlockSpec(memory_space=pl.ANY)
    block = (COLS, TB)

    def pair(*shape):
        return [pltpu.SemaphoreType.DMA(shape)] * 2

    product, gram = pl.pallas_call(
        kernel,
        out_shape=(
            jax.ShapeDtypeStruct((COLS, RB * TB), F32),
            jax.ShapeDtypeStruct((COLS, COLS * Y), F32),
        ),
        in_specs=[hbm] * 8,
        out_specs=(vmem, vmem),
        scratch_shapes=[
            pltpu.VMEM((COLS, RB * TB), BF16),
            pltpu.SMEM((RB, NB), jnp.int32),
            pltpu.SMEM((1, 2), jnp.int32),
            pltpu.VMEM((TILES, TB), BF16),
            pltpu.VMEM((1, TILES), jnp.int32),
            pltpu.VMEM((1, TILES), jnp.int32),
            pltpu.VMEM((RB * NB, TB, TB), BF16),
            pltpu.VMEM((TILES, TB, TB), BF16),
            pltpu.VMEM((RB + 8, *block), BF16),
            pltpu.VMEM((RB, *block), BF16),
            pltpu.VMEM((2, *block), BF16),
            pltpu.VMEM((FIRST, RB, *block), BF16),
            pltpu.VMEM((Z - FIRST, RB, *block), BF16),
            pltpu.VMEM((Y, COLS, RB * TB), BF16),
            pltpu.VMEM((PLANE, PLANE, TB), jnp.int32),
            pltpu.VMEM((2 * PLANE, TB), jnp.int32),
            pltpu.SMEM((PLANE, PLANE, TB), jnp.int32),
            pltpu.SMEM((2 * PLANE, TB), jnp.int32),
            pltpu.VMEM((PLANE, SLOTS, *block), BF16),
            pltpu.VMEM((PLANE, SLOTS, *block), BF16),
            pltpu.VMEM((TILES, *block), F32),
            pltpu.VMEM((PLANE, SLOTS, *block), jnp.int16),
            pltpu.VMEM((PLANE, SLOTS, *block), jnp.int16),
            pltpu.VMEM((TILES + 1, *block), jnp.int16),
            pltpu.VMEM(block, F32),
            pltpu.VMEM((PLANE, *block), F32),
            pltpu.VMEM((Z, RB, *block), F32),
            pltpu.VMEM((len(N_PLAN), RB, *block), F32),
            pltpu.VMEM((2, RB, *block), F32),
            pltpu.VMEM((4, RB, *block), F32),
            pltpu.VMEM((2, RB, *block), F32),
            pltpu.VMEM((RB, *block), F32),
            pltpu.VMEM((PLANE, 2, TB), F32),
            pltpu.VMEM((Z, 2, TB), F32),
            pltpu.VMEM((2, TB), F32),
            pltpu.VMEM((TILES, TB), F32),
            pltpu.VMEM((COLS, TILES * TB), BF16),
            pltpu.VMEM((COLS, TILES * TB), BF16),
            pltpu.VMEM((Y, COLS, TILES * TB), BF16),
            pltpu.SemaphoreType.DMA((10,)),
            *pair(len(Z_PLAN)),
            *pair(PLANE),
            *pair(Y),
            *pair(4),
            *pair(2, PLANE),
            *pair(2, PLANE),
            *pair(PLANE),
            *pair(len(N_PLAN)),
            *pair(4),
            *pair(2),
            *pair(Y),
            *pair(PLANE),
            *pair(Z),
        ],
        compiler_params=pltpu.CompilerParams(
            collective_id=0, has_side_effects=True, vmem_limit_bytes=60 * 2**20),
        name="exchange",
    )(
        x_cols, q_cols, halo_ids, obs_prec, tile_owner.reshape(1, TILES), tile_sub.reshape(1, TILES),
        q_tiles, a_tiles,
    )
    product, gram = pl.pallas_call(
        settle,
        out_shape=(jax.ShapeDtypeStruct(product.shape, F32), jax.ShapeDtypeStruct(gram.shape, F32)),
        name="settle",
    )(product, gram)
    return product, gram.T


def solution(mesh):
    torus = Mesh(mesh.devices.reshape(Z, X, C, Y), ("z", "x", "core", "col"))
    parts = ("z", "x", "core")
    in_specs = (
        P("col", parts),
        P(parts, None, None),
        P(parts, None),
        P(parts, None),
        P(parts, None, None),
        P(parts, None),
        P(parts, None),
        P(parts),
    )
    out_specs = (P("col", parts), P(None, "col"))
    return jax.shard_map(body, mesh=torus, in_specs=in_specs, out_specs=out_specs, check_vma=False)
```

```python
import math

import jax
import jax.numpy as jnp
from jax import lax
from jax.experimental import pallas as pl
from jax.experimental.pallas import tpu as pltpu
from jax.sharding import Mesh
from jax.sharding import PartitionSpec as P

LOGICAL = pl.DeviceIdType.MESH
Z, X, C, Y = 16, 4, 2, 4
PLANE = X * C
PARTS = Z * PLANE
TB = 128
COLS = 8
RB = 8
NB = 5
TILES = 64
SLOTS = 2 * Z
F32 = jnp.float32
BF16 = jnp.bfloat16
GROUP = 64
LEVELS = 32767.0
Z_PLAN = [(0, 5, None), (0, -5, None), (0, 1, None), (0, -1, None), (0, 2, None), (0, -2, None)]
Z_OWN = len(Z_PLAN)
Z_PLAN += [(-5, 3, 0), (-5, 2, None), (-5, -2, None), (-5, 1, None), (-5, -1, None)]
Z_PLAN += [(5, -3, 1), (5, 2, None), (5, -2, None), (5, 1, None), (5, -1, None)]
ORDER = (0, 1, 15, 2, 14, 5, 11, 3, 4, 6, 7, 8, 9, 10, 12, 13)
FIRST = 7
WAVES = ((0, FIRST), (FIRST, Z))
N_PLAN = [(8, -3, 0), (13, 2, None), (9, -2, None), (12, 1, None), (10, -1, None)]
N_PLAN += [(8, 3, 1), (7, 2, None), (3, -2, None), (6, 1, None), (4, -1, None)]
NT = (((1,), (1,)), ((), ()))
NN = (((1,), (0,)), ((), ()))


def kernel(
    x_hbm, qc_hbm, halo_hbm, prec_hbm, owner_hbm, sub_hbm, q_hbm, a_hbm,
    y_ref, g_ref,
    x_v, qc_s, halo_s, prec_in, own_v, sub_v,
    q_v, a_v, win, mine, share, zx, zy, xy, req, meta, req_s, meta_s, stage, xs, cb, stage2, rc,
    coded, unit_out, unit_in, dn, near, csum, direct,
    far, acc, g1, g2, gp, prec, pb, wb, pg,
    loc_sem, s_z, r_z, s_q, r_q, s_y, r_y, s_h, r_h, s_p, r_p, s_c, r_c, s_u, r_u, s_n, r_n, s_d, r_d, s_f, r_f, s_j, r_j,
    s_g1, r_g1, s_g2, r_g2,
):
    z, x, c, y = (lax.axis_index(n) for n in ("z", "x", "core", "col"))
    mq = x * C + c
    me = z * PLANE + mq

    def round_z(d):
        return lax.rem(z + d + Z, Z)

    def at_z(d):
        return {"z": round_z(d)}

    def plane_peer(k):
        px, pc = lax.rem(x + k // C, X), lax.rem(c + k % C, C)
        return {"x": px, "core": pc}, px * C + pc

    def at_part(d):
        p = lax.rem(me + d + PARTS, PARTS)
        return {"z": p // PLANE, "x": lax.rem(p // C, X), "core": lax.rem(p, C)}

    def at_y(d):
        return {"col": lax.rem(y + d, Y)}

    def send(src, dst, sems, i, where):
        return pltpu.make_async_remote_copy(
            src_ref=src, dst_ref=dst, send_sem=sems[0].at[i], recv_sem=sems[1].at[i],
            device_id=where, device_id_type=LOGICAL,
        )

    def start(copies):
        for copy in copies:
            copy.start()
        return copies

    def finish(copies):
        for copy in copies:
            copy.wait()

    loads = [
        pltpu.make_async_copy(src, dst, loc_sem.at[i])
        for i, (src, dst) in enumerate((
            (x_hbm, x_v), (halo_hbm, halo_s), (owner_hbm, own_v), (sub_hbm, sub_v), (prec_hbm, prec_in),
            (qc_hbm, qc_s), (q_hbm, q_v), (a_hbm, a_v),
        ))
    ]
    start(loads)
    x_in, halo_in, own_in, sub_in, prec_load, qc_in, q_in, a_in = loads

    barrier = pltpu.get_barrier_semaphore()
    halo_steps = (2, 1, -1, -2)
    others = [at_z(d) for d in range(1, Z)] + [plane_peer(k)[0] for k in range(1, PLANE)]
    others += [at_part(d) for d in halo_steps] + [at_y(d) for d in range(1, Y)]
    for other in others:
        pl.semaphore_signal(barrier, inc=1, device_id=other, device_id_type=LOGICAL)

    x_in.wait()
    halo_in.wait()
    for r in range(RB):
        block = x_v[:, r * TB:(r + 1) * TB]
        win[r] = block
        mine[r] = block
        zx[0, r] = block
    xy[y] = x_v[...]
    for h in range(2):
        share[h] = mine[halo_s[0, h]]

    def chunk(d):
        i = ORDER.index(d % Z)
        return zx.at[i] if i < FIRST else zy.at[i - FIRST]

    def z_copy(i):
        hold, step, half = Z_PLAN[i]
        src, dst = chunk(hold), chunk(hold - step)
        if half is not None:
            rows = pl.ds(half * (RB // 2), RB // 2)
            src, dst = src.at[rows], dst.at[rows]
        return send(src, dst, (s_z, r_z), i, at_z(step))

    z_copies = [z_copy(i) for i in range(len(Z_PLAN))]

    pl.semaphore_wait(barrier, len(others))

    start(z_copies[:Z_OWN])
    halos = start([
        send(share, win.at[pl.ds(RB + 2 * m, 2)], (s_h, r_h), m, at_part(d))
        for m, d in enumerate(halo_steps)
    ])
    probes = start([send(x_v, xy.at[y], (s_y, r_y), d, at_y(d)) for d in range(1, Y)])

    own_in.wait()
    sub_in.wait()
    prec_load.wait()
    prec[...] = prec_in[...].astype(F32)
    shape = (TILES, TB)
    lane = lax.broadcasted_iota(jnp.int32, shape, 1)
    row = lax.broadcasted_iota(jnp.int32, shape, 0)
    eye = lane == row
    fill = jnp.full((1, TB - TILES), -1, jnp.int32)
    own_r = jnp.concatenate([own_v[...], fill], axis=1)
    sub_r = jnp.concatenate([sub_v[...], fill], axis=1)
    own_b = jnp.broadcast_to(jnp.sum(jnp.where(eye, own_r, 0), axis=1, keepdims=True), shape)
    sub_b = jnp.broadcast_to(jnp.sum(jnp.where(eye, sub_r, 0), axis=1, keepdims=True), shape)
    same = own_b == own_r
    j_b = jnp.broadcast_to(
        jnp.sum(jnp.where(same & (lane < row), 1, 0), axis=1, keepdims=True), shape)
    j_r = jnp.sum(jnp.where(same & (row < lane), 1, 0), axis=0, keepdims=True)
    col_b = jnp.bitwise_and(own_b, PLANE - 1)

    def place_of(owner):
        offset = jnp.bitwise_and(jnp.right_shift(owner, 3) - z, Z - 1)
        return sum(jnp.where(offset == d, 2 * i, 0) for i, d in enumerate(ORDER) if i)

    key_b = place_of(own_b) + j_b
    for q in range(PLANE):
        hit = (col_b == q) & (key_b == lane)
        wanted = jnp.sum(jnp.where(hit, sub_b + 1, 0), axis=0, keepdims=True) - 1
        req[mq, q:q + 1] = wanted
        meta[PLANE + q:PLANE + q + 1] = jnp.sum(jnp.where(hit, row - TILES, 0), axis=0, keepdims=True) + TILES
    slot_r = jnp.bitwise_and(own_r, PLANE - 1) * SLOTS + place_of(own_r) + j_r
    meta[:PLANE] = jnp.broadcast_to(slot_r, (8, TB))
    to_meta = pltpu.make_async_copy(meta, meta_s, loc_sem.at[8])
    to_meta.start()
    asks = start([send(req.at[mq], req.at[mq], (s_q, r_q), k, plane_peer(k)[0]) for k in range(1, PLANE)])

    for i in range(2):
        z_copies[i].wait_recv()
        start(z_copies[Z_OWN + 5 * i:Z_OWN + 5 * i + 5])

    finish(asks)
    to_req = pltpu.make_async_copy(req, req_s, loc_sem.at[9])
    to_req.start()
    for copy in z_copies[2:Z_OWN]:
        copy.wait_recv()
    to_req.wait()

    def give(wave, k):
        low, high = WAVES[wave]
        slots = pl.ds(2 * low, 2 * (high - low))
        return send(stage.at[k, slots], xs.at[mq, slots], (s_p.at[wave], r_p.at[wave]), k, plane_peer(k)[0])

    def pick(wave, k, dst):
        _, q = plane_peer(k)
        held, low = (zy, FIRST) if wave else (zx, 0)
        for i in range(*WAVES[wave]):
            for j in range(2):
                dst[2 * i + j] = held[i - low, jnp.maximum(req_s[q, mq, 2 * i + j], 0)]

    for wave in range(2):
        if wave:
            for copy in z_copies[Z_OWN:]:
                copy.wait_recv()

        def hand_out(i, carry, wave=wave):
            k = lax.rem(i + 3, PLANE - 1) + 1
            pick(wave, k, stage.at[k])
            give(wave, k).start()
            return carry

        lax.fori_loop(0, PLANE - 1, hand_out, 0)
        pick(wave, 0, xs.at[mq])
    to_meta.wait()
    a_in.wait()
    for copy in z_copies:
        copy.wait_send()
    for wave in range(2):
        finish([give(wave, k) for k in range(1, PLANE)])

    xs_flat = xs.reshape(PLANE * SLOTS, COLS, TB)

    def terms(group, carry):
        base = pl.multiple_of(group * GROUP, GROUP)
        scales = prec[pl.ds(base, GROUP), :]
        tiles, projected, weighted = [], [], []
        for i in range(0, GROUP, 2):
            tile = a_v[pl.ds(base + i, 2)].reshape(2 * TB, TB)
            pair = jnp.concatenate([xs_flat[meta_s[0, base + i]], xs_flat[meta_s[0, base + i + 1]]], axis=0)
            tiles.append(tile)
            projected.append(lax.dot_general(pair, tile, NT, preferred_element_type=F32))
        zero = jnp.zeros((COLS, TB), F32)
        for i in range(0, GROUP, 2):
            both = projected[i // 2]
            top, low = both[:COLS, :TB], both[COLS:, TB:]
            top_w, low_w = scales[i:i + 1] * top, scales[i + 1:i + 2] * low
            block = jnp.concatenate([
                jnp.concatenate([top_w, zero], axis=1), jnp.concatenate([zero, low_w], axis=1)], axis=0)
            weighted.append(block.astype(BF16))
            for h, (p, w) in enumerate(((top, top_w), (low, low_w))):
                lanes = pl.ds(pl.multiple_of((base + i + h) * TB, TB), TB)
                pb[:, lanes] = p.astype(BF16)
                wb[:, lanes] = w.astype(BF16)
        for i in range(0, GROUP, 2):
            both = lax.dot_general(weighted[i // 2], tiles[i // 2], NN, preferred_element_type=F32)
            cb[base + i] = both[:COLS]
            cb[base + i + 1] = both[COLS:]
            carry = jnp.maximum(carry, jnp.maximum(jnp.abs(both[:COLS]), jnp.abs(both[COLS:])))
        return carry

    largest = lax.fori_loop(0, TILES // GROUP, terms, jnp.zeros((COLS, TB), F32))
    turns = start([send(pb, pg.at[y], (s_j, r_j), d, at_y(d)) for d in range(1, Y)])

    largest = jnp.broadcast_to(jnp.max(largest, axis=1, keepdims=True), (COLS, TB))
    unit_out[...] = largest * (1.0 / LEVELS)
    unit_in[mq] = unit_out[...]
    units = start([send(unit_out, unit_in.at[mq], (s_u, r_u), k, plane_peer(k)[0]) for k in range(1, PLANE)])
    per_unit = LEVELS / jnp.maximum(largest, 1e-30)

    def code(group, carry):
        for i in range(GROUP):
            t = group * GROUP + i
            coded[t] = jnp.floor(cb[t] * per_unit + 0.5).astype(jnp.int32).astype(jnp.int16)
        return carry

    lax.fori_loop(0, TILES // GROUP, code, 0)
    coded[TILES] = jnp.zeros((COLS, TB), jnp.int16)

    def back(wave, k):
        low, high = WAVES[wave]
        slots = pl.ds(2 * low, 2 * (high - low))
        return send(stage2.at[k, slots], rc.at[mq, slots], (s_c.at[wave], r_c.at[wave]), k, plane_peer(k)[0])

    def place(wave, k, dst):
        _, q = plane_peer(k)
        for i in range(2 * WAVES[wave][0], 2 * WAVES[wave][1]):
            dst[i] = coded[meta_s[PLANE + q, i]]

    for wave in (1, 0):

        def hand_back(i, carry, wave=wave):
            k = lax.rem(i + 3, PLANE - 1) + 1
            place(wave, k, stage2.at[k])
            back(wave, k).start()
            return carry

        lax.fori_loop(0, PLANE - 1, hand_back, 0)
        place(wave, 0, rc.at[mq])

    pg[y] = pb[...]
    finish(halos)
    qc_in.wait()
    q_in.wait()

    def prior(r, carry):
        total = jnp.zeros((COLS, TB), F32)
        for k in range(NB):
            total += lax.dot_general(win[qc_s[r, k]], q_v[r * NB + k], NT, preferred_element_type=F32)
        acc[r] = total
        return carry

    lax.fori_loop(0, RB, prior, 0, unroll=4)
    def dense(i, carry):
        totals = [jnp.zeros((COLS, TB), F32) for _ in range(RB)]
        for q in range(PLANE):
            unit = unit_in[q]
            for j in range(2):
                sub = jnp.broadcast_to(req_s[q, mq, 2 * i + j], (COLS, TB))
                block = rc[q, 2 * i + j].astype(jnp.int32).astype(F32) * unit
                totals = [total + jnp.where(sub == r, block, 0.0) for r, total in enumerate(totals)]
        for r in range(RB):
            dn[i, r] = totals[r]
        return carry

    def sums_for(d):
        return dn.at[ORDER.index(d % Z)]

    finish(units)
    finish([back(1, k) for k in range(1, PLANE)])
    lax.fori_loop(*WAVES[1], dense, 0)
    nears = []
    for i, (d, step, half) in enumerate(N_PLAN):
        src, dst = sums_for(d), near.at[i]
        if half is not None:
            rows = pl.ds(half * (RB // 2), RB // 2)
            src, dst = src.at[rows], dst.at[rows]
        nears += start([send(src, dst, (s_n, r_n), i, at_z(step))])
    finish(probes)
    part = jnp.zeros((COLS, COLS * Y), F32)
    for r in range(RB):
        across = jnp.concatenate([xy[i, :, r * TB:(r + 1) * TB] for i in range(Y)], axis=0)
        part += lax.dot_general(
            acc[r], across.astype(F32), NT, precision=lax.Precision.HIGHEST, preferred_element_type=F32)
    finish(turns)

    def gram_part(i, part):
        lanes = pl.ds(pl.multiple_of(i * 1024, 1024), 1024)
        across = jnp.concatenate([pg[j, :, lanes] for j in range(Y)], axis=0)
        return part + lax.dot_general(wb[:, lanes], across, NT, preferred_element_type=F32)

    part = lax.fori_loop(0, TILES * TB // 1024, gram_part, part)
    gp[...] = jnp.concatenate([part[2 * i:2 * i + 2] for i in range(COLS // 2)], axis=1)
    firsts = start([send(gp, g1.at[k], (s_g1, r_g1), k, plane_peer(k)[0]) for k in range(1, PLANE)])
    g1[0] = gp[...]

    finish([back(0, k) for k in range(1, PLANE)])
    lax.fori_loop(*WAVES[0], dense, 0)
    directs = start([send(sums_for(d), direct.at[i], (s_d, r_d), i, at_z(d)) for i, d in enumerate((1, -1, 2, -2))])
    finish(firsts)
    g2[0] = jnp.sum(g1[...], axis=0)
    seconds = start([send(g2.at[0], g2.at[d], (s_g2, r_g2), d, at_z(d)) for d in range(1, Z)])
    finish(nears)
    fars = []
    for g, d in enumerate((-5, 5)):
        for r in range(RB):
            total = sums_for(d)[r]
            for i in range(4):
                total += near[5 * g + 1 + i, r]
            if r // (RB // 2) == g:
                total += near[5 * g, r]
            csum[g, r] = total
        fars += start([send(csum.at[g], far.at[g], (s_f, r_f), g, at_z(d))])
    finish(directs)
    for r in range(RB):
        acc[r] += (dn[0, r] + direct[0, r]) + (direct[1, r] + direct[2, r]) + direct[3, r]
    finish(seconds)
    total = jnp.sum(g2[...], axis=0) * (1.0 / math.sqrt(RB * TB * PARTS))
    width = COLS * Y
    g_ref[...] = jnp.concatenate([total[:, i * width:(i + 1) * width] for i in range(COLS // 2)], axis=0)
    finish(fars)
    for r in range(RB):
        y_ref[:, r * TB:(r + 1) * TB] = acc[r] + (far[0, r] + far[1, r])


def settle(product_ref, gram_ref, y_ref, g_ref):
    y_ref[...] = product_ref[...]
    g_ref[...] = gram_ref[...]


def body(x_cols, q_tiles, q_cols, halo_ids, a_tiles, obs_prec, tile_owner, tile_sub):
    vmem = pl.BlockSpec(memory_space=pltpu.VMEM)
    hbm = pl.BlockSpec(memory_space=pl.ANY)
    block = (COLS, TB)

    def pair(*shape):
        return [pltpu.SemaphoreType.DMA(shape)] * 2

    product, gram = pl.pallas_call(
        kernel,
        out_shape=(
            jax.ShapeDtypeStruct((COLS, RB * TB), F32),
            jax.ShapeDtypeStruct((COLS, COLS * Y), F32),
        ),
        in_specs=[hbm] * 8,
        out_specs=(vmem, vmem),
        scratch_shapes=[
            pltpu.VMEM((COLS, RB * TB), BF16),
            pltpu.SMEM((RB, NB), jnp.int32),
            pltpu.SMEM((1, 2), jnp.int32),
            pltpu.VMEM((TILES, TB), BF16),
            pltpu.VMEM((1, TILES), jnp.int32),
            pltpu.VMEM((1, TILES), jnp.int32),
            pltpu.VMEM((RB * NB, TB, TB), BF16),
            pltpu.VMEM((TILES, TB, TB), BF16),
            pltpu.VMEM((RB + 8, *block), BF16),
            pltpu.VMEM((RB, *block), BF16),
            pltpu.VMEM((2, *block), BF16),
            pltpu.VMEM((FIRST, RB, *block), BF16),
            pltpu.VMEM((Z - FIRST, RB, *block), BF16),
            pltpu.VMEM((Y, COLS, RB * TB), BF16),
            pltpu.VMEM((PLANE, PLANE, TB), jnp.int32),
            pltpu.VMEM((2 * PLANE, TB), jnp.int32),
            pltpu.SMEM((PLANE, PLANE, TB), jnp.int32),
            pltpu.SMEM((2 * PLANE, TB), jnp.int32),
            pltpu.VMEM((PLANE, SLOTS, *block), BF16),
            pltpu.VMEM((PLANE, SLOTS, *block), BF16),
            pltpu.VMEM((TILES, *block), F32),
            pltpu.VMEM((PLANE, SLOTS, *block), jnp.int16),
            pltpu.VMEM((PLANE, SLOTS, *block), jnp.int16),
            pltpu.VMEM((TILES + 1, *block), jnp.int16),
            pltpu.VMEM(block, F32),
            pltpu.VMEM((PLANE, *block), F32),
            pltpu.VMEM((Z, RB, *block), F32),
            pltpu.VMEM((len(N_PLAN), RB, *block), F32),
            pltpu.VMEM((2, RB, *block), F32),
            pltpu.VMEM((4, RB, *block), F32),
            pltpu.VMEM((2, RB, *block), F32),
            pltpu.VMEM((RB, *block), F32),
            pltpu.VMEM((PLANE, 2, TB), F32),
            pltpu.VMEM((Z, 2, TB), F32),
            pltpu.VMEM((2, TB), F32),
            pltpu.VMEM((TILES, TB), F32),
            pltpu.VMEM((COLS, TILES * TB), BF16),
            pltpu.VMEM((COLS, TILES * TB), BF16),
            pltpu.VMEM((Y, COLS, TILES * TB), BF16),
            pltpu.SemaphoreType.DMA((10,)),
            *pair(len(Z_PLAN)),
            *pair(PLANE),
            *pair(Y),
            *pair(4),
            *pair(2, PLANE),
            *pair(2, PLANE),
            *pair(PLANE),
            *pair(len(N_PLAN)),
            *pair(4),
            *pair(2),
            *pair(Y),
            *pair(PLANE),
            *pair(Z),
        ],
        compiler_params=pltpu.CompilerParams(
            collective_id=0, has_side_effects=True, vmem_limit_bytes=60 * 2**20),
        name="exchange",
    )(
        x_cols, q_cols, halo_ids, obs_prec, tile_owner.reshape(1, TILES), tile_sub.reshape(1, TILES),
        q_tiles, a_tiles,
    )
    product, gram = pl.pallas_call(
        settle,
        out_shape=(jax.ShapeDtypeStruct(product.shape, F32), jax.ShapeDtypeStruct(gram.shape, F32)),
        name="settle",
    )(product, gram)
    return product, gram.T


def solution(mesh):
    torus = Mesh(mesh.devices.reshape(Z, X, C, Y), ("z", "x", "core", "col"))
    parts = ("z", "x", "core")
    in_specs = (
        P("col", parts),
        P(parts, None, None),
        P(parts, None),
        P(parts, None),
        P(parts, None, None),
        P(parts, None),
        P(parts, None),
        P(parts),
    )
    out_specs = (P("col", parts), P(None, "col"))
    return jax.shard_map(body, mesh=torus, in_specs=in_specs, out_specs=out_specs, check_vma=False)
```
